512 devices in a mesh: seq: 128 (over z, y, core), head: 4 (over x).
Axes of the slice: x: 4, y: 4, z: 16, core: 2. Of those that a mesh axis runs over, the one named last changes fastest.
Arguments:
- patches: bfloat16 [32768, 1280], P('seq'), may hold values from -6 to 6
- norm_gain: float32 [1280], replicated, may hold values from 0.5 to 1.5
- w_qkv: bfloat16 [1280, 3, 1280], P('seq', None, 'head'), as said below
- w_out: bfloat16 [1280, 1280], P('head', 'seq'), may hold values from -0.15625 to 0.15625
- window_order: int32 [128, 64], P('seq'), may hold values from 0 to 63, each once within a row
- merge_gain: float32 [1280], replicated, may hold values from 0.5 to 1.5
- w_kv: bfloat16 [5120, 2, 1024], P('seq', None, 'head'), as said below
- queries: bfloat16 [256, 8192], P('seq', 'head'), may hold values from -6 to 6
- suffix_kv: bfloat16 [256, 64, 2, 1024], P('seq', None, None, 'head'), may hold values from -12 to 12
- question_lengths: int32 [256], P('seq'), may hold values from 1 to 64
- frame_range: int32 [256, 2], replicated, may hold values from 0 to 128, as said below
Outputs:
- answers: bfloat16 [256, 8192], P('seq', 'head')
The draws below stay inside these ranges and needn't reach their ends.
Inputs may be any that keep to these rules, and one draw needn't show every extreme that they name: `window_order`: each row is an ordering of a frame's units; positions w * 16 to (w + 1) * 16 - 1 form window w. `frame_range`: the first entry of a row is below the second. `w_qkv`: entries of order one over the square root of 1280. `w_kv`: entries of order one over the square root of 5120.
All inputs are finite; a program needn't handle non-finite values.
Results may differ from the reference program's by a relative error of at most 0.007.
Values may be sent and summed in bfloat16 or wider, within the bound.
No kernel may reach another device: no remote copies, remote signals or barrier semaphores. Data moves between devices by JAX's collectives and lax.ppermute only.
A program may use at most 64 MiB of HBM per device.

```python
import math
import jax
import jax.numpy as jnp
from jax import lax

VD = 1280
VH = 16
QH = 64
KVH = 8
HD = 128
FPATCH = 256
WIN = 64
SUF = 64
FRAMES = 128
PATCHES = 32768
QUESTIONS = 256


def draw_frame_range(key, part):
    first_key, second_key = jax.random.split(jax.random.fold_in(key, 11))
    first_pick = jax.random.randint(first_key, (QUESTIONS,), 0, FRAMES)
    second_pick = jax.random.randint(second_key, (QUESTIONS,), 0, FRAMES)
    lower = jnp.minimum(first_pick, second_pick)
    upper = jnp.maximum(first_pick, second_pick) + 1
    return jnp.stack([lower, upper], axis=1).astype(jnp.int32)


def sign_vector(seed_key, count):
    return jnp.where(jax.random.bernoulli(seed_key, 0.5, (count,)), 1.0, -1.0).astype(jnp.float32)


def plant_plan(seed_key):
    subkeys = jax.random.split(jax.random.fold_in(seed_key, 29), 6)
    vision_levels = jnp.linspace(100.0, 400.0, VH)
    prefix_levels = jnp.linspace(100.0, 480.0, KVH)
    head_width = VD // VH
    vision_alpha = jnp.sqrt(jax.random.permutation(subkeys[0], vision_levels) / (VD * math.sqrt(head_width)))
    prefix_alpha = jax.random.permutation(subkeys[1], prefix_levels) / (6.0 * math.sqrt(4 * VD * HD))
    vision_sign = sign_vector(subkeys[2], VD)
    vision_dir = sign_vector(subkeys[3], VD)
    prefix_sign = sign_vector(subkeys[4], 4 * VD)
    prefix_dir = sign_vector(subkeys[5], KVH * HD)
    return (vision_alpha, vision_sign, vision_dir, prefix_alpha, prefix_sign, prefix_dir)


def draw_patches(key, part):
    vision_alpha, vision_sign, vision_dir, prefix_alpha, prefix_sign, prefix_dir = plant_plan(key)
    subkeys = jax.random.split(jax.random.fold_in(key, 37), 9)
    background = jnp.clip(jax.random.normal(subkeys[1], (PATCHES, VD), jnp.float32), -6.0, 6.0)
    unit_count = FPATCH // 4
    frame_keys = jax.random.split(subkeys[2], FRAMES)
    chosen = jax.vmap(lambda frame_key: jax.random.permutation(frame_key, unit_count)[:3])(frame_keys)
    vision_field = jax.random.uniform(subkeys[3], (FRAMES, 1, VD), jnp.float32)
    vision_noise = jnp.clip(jax.random.normal(subkeys[4], (FRAMES, 1, VD), jnp.float32), -6.0, 6.0)
    vision_base = jax.random.uniform(subkeys[5], (FRAMES, 1, 1), jnp.float32, 0.0, 0.2)
    thresholds = vision_base + 0.01 * jnp.arange(4, dtype=jnp.float32).reshape(1, 4, 1)
    vision_unit = jnp.where(vision_field < thresholds, vision_noise, 6.0 * vision_sign.reshape(1, 1, VD))
    prefix_field = jax.random.uniform(subkeys[6], (FRAMES, 4, VD), jnp.float32)
    prefix_noise = jnp.clip(jax.random.normal(subkeys[7], (FRAMES, 4, VD), jnp.float32), -6.0, 6.0)
    prefix_base = jax.random.uniform(subkeys[8], (FRAMES, 1, 1), jnp.float32, 0.0, 0.25)
    pattern = 6.0 * prefix_sign.reshape(1, 4, VD)
    first_unit = jnp.where(prefix_field < prefix_base, prefix_noise, pattern)
    second_unit = jnp.where(prefix_field < prefix_base + 0.01, prefix_noise, pattern)
    frame_ids = jnp.arange(FRAMES)
    layout = background.reshape(FRAMES, unit_count, 4, VD)
    layout = layout.at[frame_ids, chosen[:, 0]].set(vision_unit)
    layout = layout.at[frame_ids, chosen[:, 1]].set(first_unit)
    layout = layout.at[frame_ids, chosen[:, 2]].set(second_unit)
    return layout.reshape(PATCHES, VD).astype(jnp.bfloat16)


def draw_w_qkv(key, part):
    vision_alpha, vision_sign, vision_dir, prefix_alpha, prefix_sign, prefix_dir = plant_plan(key)
    weight_key = jax.random.fold_in(key, 41)
    random_part = jnp.clip(jax.random.normal(weight_key, (VD, 3, VD), jnp.float32), -4.0, 4.0) * VD ** (-0.5)
    column_alpha = jnp.repeat(vision_alpha, VD // VH)
    rank_one = vision_sign[:, None] * (column_alpha * vision_dir)[None, :] * VD ** (-0.5)
    planted = jnp.stack([rank_one, rank_one, jnp.zeros_like(rank_one)], axis=1)
    return (random_part + planted).astype(jnp.bfloat16)


def draw_w_kv(key, part):
    vision_alpha, vision_sign, vision_dir, prefix_alpha, prefix_sign, prefix_dir = plant_plan(key)
    weight_key = jax.random.fold_in(key, 43)
    random_part = jnp.clip(jax.random.normal(weight_key, (4 * VD, 2, KVH * HD), jnp.float32), -4.0, 4.0) * (4 * VD) ** (-0.5)
    column_alpha = jnp.repeat(prefix_alpha, HD)
    rank_one = prefix_sign[:, None] * (column_alpha * prefix_dir)[None, :] * (4 * VD) ** (-0.5)
    planted = jnp.stack([rank_one, jnp.zeros_like(rank_one)], axis=1)
    return (random_part + planted).astype(jnp.bfloat16)


def draw_queries(key, part):
    vision_alpha, vision_sign, vision_dir, prefix_alpha, prefix_sign, prefix_dir = plant_plan(key)
    subkeys = jax.random.split(jax.random.fold_in(key, 47), 3)
    background = jnp.clip(jax.random.normal(subkeys[0], (QUESTIONS, QH, HD), jnp.float32), -6.0, 6.0)
    chosen = jax.random.bernoulli(subkeys[1], 0.25, (QUESTIONS, QH))
    levels = jnp.array([1.5, 3.0, 6.0, 6.0], jnp.float32)
    strength = levels[jax.random.randint(subkeys[2], (QUESTIONS, QH), 0, 4)]
    direction = jnp.broadcast_to(prefix_dir.reshape(KVH, 1, HD), (KVH, QH // KVH, HD)).reshape(QH, HD)
    planted = strength[..., None] * direction[None]
    shaped = jnp.where(chosen[..., None], planted, background)
    return shaped.reshape(QUESTIONS, QH * HD).astype(jnp.bfloat16)


def touch_ends(entries, stream_key, low, largest):
    shape = entries.shape
    place = [jax.random.randint(jax.random.fold_in(stream_key, axis), (), 0, shape[axis]) for axis in range(len(shape))]
    entries = entries.at[tuple(place)].set(low)
    longest = shape.index(max(shape))
    place[longest] = (place[longest] + 1) % shape[longest]
    return entries.at[tuple(place)].set(largest)


def level_of(rng, shape, shards, least, largest):
    level = 1.0
    for axis_at, shards_of in shards:
        heights = jax.random.uniform(jax.random.fold_in(jax.random.fold_in(rng, 6), axis_at), (shards_of,), jnp.float32, least / len(shards), largest / len(shards))
        level = level * jnp.repeat(jnp.exp(heights), shape[axis_at] // shards_of).reshape((-1,) + (1,) * (len(shape) - 1 - axis_at))
    return level


def normal_values(key, dims, deviation, limit, pieces=(), held_as=jnp.bfloat16):
    entries = deviation * jax.random.normal(key, dims, jnp.float32)
    if pieces:
        entries = entries * level_of(key, dims, pieces, -0.22, 0.18)
    return jnp.clip(entries, -limit, limit).astype(held_as)


def setup_inputs(seed: int = 0) -> dict:
    key_list = jax.random.split(jax.random.key(seed), 12)
    patches = draw_patches(jax.random.fold_in(key_list[11], 71), 0)
    norm_gain = jnp.clip(1.0 + 0.1 * jax.random.normal(key_list[1], (VD,), jnp.float32), 0.5, 1.5)
    w_qkv = draw_w_qkv(jax.random.fold_in(key_list[11], 71), 0)
    w_out = normal_values(key_list[3], (VD, VD), VD ** -0.5, 0.15625, ((0, 4), (1, 128)))
    window_order = jax.vmap(lambda own: jax.random.permutation(own, FPATCH // 4))(jax.random.split(key_list[4], FRAMES)).reshape((FRAMES, FPATCH // 4)).astype(jnp.int32)
    merge_gain = jnp.clip(1.0 + 0.1 * jax.random.normal(key_list[5], (VD,), jnp.float32), 0.5, 1.5)
    w_kv = draw_w_kv(jax.random.fold_in(key_list[11], 71), 0)
    queries = draw_queries(jax.random.fold_in(key_list[11], 71), 0)
    suffix_kv = normal_values(key_list[8], (QUESTIONS, SUF, 2, KVH * HD), 2.0, 12.0, ((0, 128), (3, 4)))
    question_lengths = touch_ends(jax.random.randint(key_list[9], (QUESTIONS,), 1, SUF + 1), jax.random.fold_in(key_list[9], 1), 1, SUF).astype(jnp.int32)
    frame_range = draw_frame_range(jax.random.fold_in(key_list[11], 71), 0)
    return {"patches": patches, "norm_gain": norm_gain, "w_qkv": w_qkv, "w_out": w_out, "window_order": window_order, "merge_gain": merge_gain, "w_kv": w_kv, "queries": queries, "suffix_kv": suffix_kv, "question_lengths": question_lengths, "frame_range": frame_range}


def rms_scale(values, gain):
    return values * lax.rsqrt(lax.optimization_barrier(jnp.mean(values * values, axis=-1, keepdims=True)) + 1e-06) * gain

def reference(patches, norm_gain, w_qkv, w_out, window_order, merge_gain, w_kv, queries, suffix_kv, question_lengths, frame_range):
    head_size = VD // VH
    source = patches.astype(jnp.float32)
    normed = rms_scale(source, norm_gain).astype(jnp.bfloat16)
    projected = jnp.dot(normed, w_qkv.reshape(VD, 3 * VD), preferred_element_type=jnp.float32).astype(jnp.bfloat16)
    projected = projected.reshape(FRAMES, FPATCH // 4, 4, 3, VD)

    def frame_window(inputs):
        frame_rows, unit_order = inputs
        grouped = frame_rows[unit_order].reshape(-1, WIN, 3, VH, head_size).astype(jnp.float32)
        scores = jnp.einsum('wqhd,wkhd->whqk', grouped[:, :, 0], grouped[:, :, 1]) * head_size ** (-0.5)
        weights = jax.nn.softmax(scores, axis=-1).astype(jnp.bfloat16)
        weights = lax.optimization_barrier(weights).astype(jnp.float32)
        mixed = jnp.einsum('whqk,wkhd->wqhd', weights, grouped[:, :, 2]).astype(jnp.bfloat16)
        mixed = mixed.reshape(FPATCH // 4, 4, VD)
        return jnp.zeros_like(mixed).at[unit_order].set(mixed)
    attended = lax.map(frame_window, (projected, window_order)).reshape(PATCHES, VD)
    hidden = source + jnp.dot(attended, w_out, preferred_element_type=jnp.float32)
    merged = rms_scale(hidden, merge_gain).astype(jnp.bfloat16).reshape(PATCHES // 4, 4 * VD)
    visual = jnp.dot(merged, w_kv.reshape(4 * VD, 2 * KVH * HD), preferred_element_type=jnp.float32).astype(jnp.bfloat16)
    visual = visual.reshape(PATCHES // 4, 2, KVH, HD).astype(jnp.float32)
    prefix_keys = visual[:, 0]
    prefix_values = visual[:, 1]
    frame_index = jnp.arange(PATCHES // 4) // (FPATCH // 4)
    group = QH // KVH

    def answer(inputs):
        query_row, suffix_rows, length, bounds = inputs
        asking = query_row.reshape(KVH, group, HD).astype(jnp.float32)
        suffix_rows = suffix_rows.reshape(SUF, 2, KVH, HD).astype(jnp.float32)
        keys = jnp.concatenate([prefix_keys, suffix_rows[:, 0]], axis=0)
        values = jnp.concatenate([prefix_values, suffix_rows[:, 1]], axis=0)
        live = jnp.concatenate([(frame_index >= bounds[0]) & (frame_index < bounds[1]), jnp.arange(SUF) < length])
        scores = jnp.einsum('gjd,ngd->gjn', asking, keys) * HD ** (-0.5)
        scores = jnp.where(live[None, None, :], scores, -jnp.inf)
        weights = jnp.exp(scores - lax.optimization_barrier(jnp.max(scores, axis=-1, keepdims=True)))
        totals = lax.optimization_barrier(jnp.sum(weights, axis=-1))
        rounded = lax.optimization_barrier(weights.astype(jnp.bfloat16)).astype(jnp.float32)
        mixed = jnp.einsum('gjn,ngd->gjd', rounded, values) / totals[..., None]
        return mixed.reshape(QH * HD).astype(jnp.bfloat16)
    return lax.map(answer, (queries, suffix_kv, question_lengths, frame_range))
```

```python
import functools

import jax
import jax.numpy as jnp
import numpy as np
from jax import lax
from jax.experimental import pallas as pl
from jax.experimental.pallas import tpu as pltpu
from jax.sharding import Mesh
from jax.sharding import PartitionSpec as P

VD = 1280
VH = 16
HD = 128
FPATCH = 256
WIN = 64
SEQ = ("seq_0", "seq_1", "seq_2")
NZ, NY, NC, NX = 16, 4, 2, 4
ROWS = VD // (NZ * NY * NC)
COLS = VD // NX
HEAD = VD // VH
HEADS = COLS // HEAD
UNITS = FPATCH // 4
GROUP = 8
LAYER = NY * NC
NEGATIVE = -1e30
f32 = jnp.float32
bf16 = jnp.bfloat16


def dot(a, b):
    return lax.dot_general(a, b, (((1,), (0,)), ((), ())), preferred_element_type=f32)


def dot_t(a, b):
    return lax.dot_general(a, b, (((1,), (1,)), ((), ())), preferred_element_type=f32)


def iota(shape, dim):
    return lax.broadcasted_iota(jnp.int32, shape, dim)


def one_hot(condition):
    return jnp.where(condition, 1.0, 0.0).astype(bf16)


def row_order():
    order = np.zeros((VD, VD), np.float32)
    z, y, c, r = np.meshgrid(np.arange(NZ), np.arange(NY), np.arange(NC), np.arange(ROWS), indexing="ij")
    order[((z * NY + y) * NC + c) * ROWS + r, ((c * NY + y) * NZ + z) * ROWS + r] = 1.0
    return order


def copies_over(value, axes, count):
    copies = jnp.broadcast_to(value[None], (count, *value.shape))
    return lax.all_to_all(copies, axes, split_axis=0, concat_axis=0, tiled=True)


def call(body, outs, operands, specs=None, vmem=40 << 20):
    vm = pl.BlockSpec(memory_space=pltpu.VMEM)
    return pl.pallas_call(
        body,
        out_shape=outs,
        in_specs=specs or [vm] * len(operands),
        out_specs=jax.tree.map(lambda _: vm, outs),
        compiler_params=pltpu.CompilerParams(vmem_limit_bytes=vmem),
    )(*operands)


VMEM = pl.BlockSpec(memory_space=pltpu.VMEM)
SMEM = pl.BlockSpec(memory_space=pltpu.SMEM)


def compact_kernel(got_ref, weights_ref, asked_ref):
    got = got_ref[...]
    shape = (NZ * ROWS, NZ * 16)
    row, col = iota(shape, 0), iota(shape, 1)
    pick = one_hot(col == (row // ROWS) * 16 + row % ROWS)
    weights = dot(pick, got).astype(bf16)
    for k in range(NY):
        weights_ref[k] = weights
    shape = (NZ * 4, NZ * 16)
    row, col = iota(shape, 0), iota(shape, 1)
    pick = one_hot(col == (row // 4) * 16 + ROWS + row % 4)
    asked_ref[...] = dot(pick, got[:, : GROUP * HD]).astype(bf16)


def vision_kernel(core_ref, patches_ref, gain_ref, own_ref, other_ref, window_ref, order_ref, out_ref):
    first = core_ref[0] == 0
    source = patches_ref[...].astype(f32)
    scale = lax.rsqrt(jnp.mean(source * source, axis=-1, keepdims=True) + 1e-06)
    normed = (source * scale * gain_ref[...]).astype(bf16)
    normed = dot(normed, order_ref[...]).astype(bf16)
    half = VD // 2
    left, right = normed[:, :half], normed[:, half:]
    mine = jnp.where(first, left.astype(f32), right.astype(f32)).astype(bf16)
    theirs = jnp.where(first, right.astype(f32), left.astype(f32)).astype(bf16)
    wide = 1024
    projected = dot(mine, own_ref[:, :wide]) + dot(theirs, other_ref[:, :wide])
    projected = projected.astype(bf16).astype(f32)
    query = pltpu.roll(projected[:, 0:384], 64, 1)
    key = projected[:, 256:640].astype(bf16)
    value = projected[:, 640:1024]
    shape = (FPATCH, UNITS)
    member = one_hot(window_ref[...] == iota(shape, 0) // 4)
    shape = (UNITS, 128)
    member = dot(member, one_hot(iota(shape, 0) // (WIN // 4) == iota(shape, 1))).astype(bf16)
    together = dot_t(member, member) > 0.5
    lane = iota((1, 384), 1)
    mixed = jnp.zeros((FPATCH, 384), f32)
    for h in range(HEADS):
        at = 64 + h * HEAD
        asking = jnp.where((lane >= at) & (lane < at + HEAD), query, 0.0).astype(bf16)
        scores = dot_t(asking, key) * HEAD ** (-0.5)
        scores = jnp.where(together, scores, NEGATIVE)
        weights = jnp.exp(scores - jnp.max(scores, axis=-1, keepdims=True))
        weights = (weights / jnp.sum(weights, axis=-1, keepdims=True)).astype(bf16)
        at = h * HEAD
        mixed += dot(weights, jnp.where((lane >= at) & (lane < at + HEAD), value, 0.0).astype(bf16))
    mixed = pltpu.roll(mixed, 64, 1).astype(bf16)
    shape = (FPATCH, FPATCH)
    row, col = iota(shape, 0), iota(shape, 1)
    mixed = dot(one_hot(col == (row % UNITS) * 4 + row // UNITS), mixed).astype(bf16)
    mine = dot_t(mixed, own_ref[:, 896:1280])
    theirs = dot_t(mixed, other_ref[:, 896:1280])
    left = jnp.where(first, mine, theirs)
    right = jnp.where(first, theirs, mine)
    summed = jnp.concatenate([left, right], axis=1).astype(bf16)
    out_ref[...] = dot_t(summed, order_ref[...]).astype(bf16)


def merge_kernel(place_ref, got_ref, patches_ref, gain_ref, out_ref):
    shape = (UNITS, FPATCH)
    pick = one_hot(iota(shape, 1) == iota(shape, 0) * 4 + place_ref[0])
    hidden = jnp.zeros((UNITS, VD), f32)
    for k in range(NX):
        hidden += got_ref[k * UNITS : (k + 1) * UNITS].astype(f32)
    hidden += dot(pick, patches_ref[...])
    scale = lax.rsqrt(jnp.mean(hidden * hidden, axis=-1, keepdims=True) + 1e-06)
    out_ref[...] = (hidden * scale * gain_ref[...]).astype(bf16)


def visual_kernel(merged_ref, weights_ref, out_ref, total_ref):
    step = pl.program_id(0)
    part = dot(merged_ref[...], weights_ref[...])

    @pl.when(step == 0)
    def _():
        total_ref[...] = part

    @pl.when(step > 0)
    def _():
        total_ref[...] += part

    @pl.when(step == 3)
    def _():
        visual = total_ref[...].astype(bf16)
        for k in range(LAYER):
            out_ref[k] = visual


def project_visual(merged, weights):
    return pl.pallas_call(
        visual_kernel,
        grid=(4,),
        in_specs=[
            pl.BlockSpec((UNITS, VD), lambda i: (i, 0)),
            pl.BlockSpec((VD, 512), lambda i: (i, 0)),
        ],
        out_specs=pl.BlockSpec((LAYER, UNITS, 512), lambda i: (0, 0, 0)),
        out_shape=jax.ShapeDtypeStruct((LAYER, UNITS, 512), bf16),
        scratch_shapes=[pltpu.VMEM((UNITS, 512), f32)],
        compiler_params=pltpu.CompilerParams(vmem_limit_bytes=40 << 20),
    )(merged, weights)


def attend_kernel(place_ref, visual_ref, asked_ref, range_ref, out_ref):
    layer, inner = place_ref[0], place_ref[1]
    count = NZ * 4 * GROUP
    tokens = LAYER * UNITS
    asking = jnp.concatenate([asked_ref[:, j * HD : (j + 1) * HD] for j in range(GROUP)], axis=0)
    row = iota((count, 1), 0)
    even = row % 2 == 0
    question = (((row // 4) % NZ) * LAYER + inner) * 2 + (row // 2) % 2
    pick = one_hot(iota((count, 256), 1) == question)
    bounds = dot(pick, range_ref[...].astype(f32).astype(bf16))
    lower, upper = bounds[:, 0:1], bounds[:, 1:2]
    frame = (layer * LAYER + iota((1, tokens), 1) // UNITS).astype(f32)
    live = (frame >= lower) & (frame < upper)
    scores = jnp.where(even, dot_t(asking, visual_ref[:, 0:128]), dot_t(asking, visual_ref[:, 128:256]))
    scores = jnp.where(live, scores * HD ** (-0.5), NEGATIVE)
    highest = jnp.max(scores, axis=-1, keepdims=True)
    weights = jnp.exp(scores - highest)
    total = jnp.sum(weights, axis=-1, keepdims=True)
    weights = weights.astype(bf16)
    mixed = jnp.where(even, dot(weights, visual_ref[:, 256:384]), dot(weights, visual_ref[:, 384:512]))
    mixed = mixed / total
    level = highest + jnp.log(total)
    high = level.astype(bf16).astype(f32)
    middle = (level - high).astype(bf16).astype(f32)
    low = level - high - middle
    lane = iota((1, HD), 1)
    levels = jnp.where(lane == 0, high, jnp.where(lane == 1, middle, jnp.where(lane == 2, low, 0.0)))
    sent = jnp.concatenate([mixed, levels], axis=1).astype(bf16)
    shape = (count, count)
    row, col = iota(shape, 0), iota(shape, 1)
    order = one_hot(col == (row % GROUP) * (NZ * 4) + row // GROUP)
    out_ref[...] = dot(order, sent).astype(bf16)


def answer_kernel(length_ref, got_ref, asking_ref, suffix_ref, out_ref):
    asking = asking_ref[...]
    count = asking.shape[0]
    span = suffix_ref.shape[0] // 2
    row = iota((count, 1), 0)
    even = (row // GROUP) % 2 == 0
    second = row // (2 * GROUP)
    scores = jnp.where(even, dot_t(asking, suffix_ref[:, 0:128]), dot_t(asking, suffix_ref[:, 128:256]))
    col = iota((1, 2 * span), 1)
    length = jnp.where(second == 0, length_ref[0], length_ref[1])
    live = (col // span == second) & (col % span < length)
    scores = jnp.where(live, scores * HD ** (-0.5), NEGATIVE)
    highest = jnp.max(scores, axis=-1, keepdims=True)
    weights = jnp.exp(scores - highest)
    total = jnp.sum(weights, axis=-1, keepdims=True)
    weights = weights.astype(bf16)
    mixed = jnp.where(even, dot(weights, suffix_ref[:, 256:384]), dot(weights, suffix_ref[:, 384:512]))
    levels = []
    top = highest
    for k in range(NZ):
        parts = got_ref[k * count : (k + 1) * count, HD:].astype(f32)
        level = parts[:, 0:1] + parts[:, 1:2] + parts[:, 2:3]
        levels.append(level)
        top = jnp.maximum(top, level)
    share = jnp.exp(highest - top)
    mixed = mixed * share
    total = total * share
    for k in range(NZ):
        share = jnp.exp(levels[k] - top)
        mixed += got_ref[k * count : (k + 1) * count, :HD].astype(f32) * share
        total += share
    out_ref[...] = (mixed / total).astype(bf16)


def on_device(
    patches,
    norm_gain,
    w_qkv,
    w_out,
    window_order,
    merge_gain,
    w_kv,
    queries,
    suffix_kv,
    question_lengths,
    frame_range,
):
    sds = jax.ShapeDtypeStruct
    layer = lax.axis_index("seq_0")
    inner = lax.axis_index(("seq_1", "seq_2"))
    core = lax.axis_index("seq_2")
    place = lax.axis_index("head")

    near = copies_over(w_kv.reshape(-1, 512), ("seq_1", "seq_2"), LAYER).reshape(-1, 512)
    packed = jnp.concatenate([w_qkv.reshape(ROWS, 3 * COLS), w_out.T], axis=1)
    asking = jnp.pad(queries.reshape(4, GROUP * HD), ((0, 2), (0, VD - GROUP * HD)))
    packed = jnp.concatenate([packed, asking], axis=0)
    packed, near = lax.optimization_barrier((packed, near))
    kv_weights = lax.all_gather(near, "seq_0", axis=0, tiled=True)

    got = copies_over(packed, "seq_0", NZ).reshape(NZ * 16, VD)
    weights, asked = call(
        compact_kernel,
        (sds((NY, NZ * ROWS, VD), bf16), sds((NZ * 4, GROUP * HD), bf16)),
        (got,),
    )
    own = lax.all_to_all(weights, "seq_1", split_axis=0, concat_axis=0, tiled=True).reshape(VD // 2, VD)
    other = lax.ppermute(own, "seq_2", [(0, 1), (1, 0)])
    order = jnp.asarray(row_order(), bf16)
    partial = call(
        vision_kernel,
        sds((FPATCH, VD), bf16),
        (core.reshape(1), patches, norm_gain.reshape(1, VD), own, other, window_order, order),
        [SMEM] + [VMEM] * 6,
    )
    partial = lax.all_to_all(
        partial.reshape(NX, UNITS, VD), "head", split_axis=0, concat_axis=0, tiled=True
    ).reshape(FPATCH, VD)
    merged = call(
        merge_kernel,
        sds((UNITS, VD), bf16),
        (place.reshape(1), partial, patches, merge_gain.reshape(1, VD)),
        [SMEM] + [VMEM] * 3,
    )
    merged = lax.all_gather(merged, "head", axis=0, tiled=True)
    visual = project_visual(merged, kv_weights)
    visual = lax.all_to_all(
        visual, ("seq_1", "seq_2"), split_axis=0, concat_axis=0, tiled=True
    ).reshape(LAYER * UNITS, 512)
    sent = call(
        attend_kernel,
        sds((NZ * 4 * GROUP, 2 * HD), bf16),
        (jnp.stack([layer, inner]), visual, asked, frame_range),
        [SMEM] + [VMEM] * 3,
    )
    got = lax.all_to_all(
        sent.reshape(NZ, 4 * GROUP, 2 * HD), "seq_0", split_axis=0, concat_axis=0, tiled=True
    ).reshape(-1, 2 * HD)
    answers = call(
        answer_kernel,
        sds((4 * GROUP, HD), bf16),
        (question_lengths, got, queries.reshape(4 * GROUP, HD), suffix_kv.reshape(-1, 512)),
        [SMEM] + [VMEM] * 3,
    )
    return answers.reshape(2, -1)


def solution(mesh):
    torus = Mesh(
        mesh.devices.reshape(NZ, NY, NC, NX), ("seq_0", "seq_1", "seq_2", "head")
    )
    in_specs = (
        P(SEQ, None),
        P(),
        P(SEQ, None, "head"),
        P("head", SEQ),
        P(SEQ, None),
        P(),
        P(SEQ, None, "head"),
        P(SEQ, "head"),
        P(SEQ, None, None, "head"),
        P(SEQ),
        P(),
    )
    return jax.shard_map(
        on_device, mesh=torus, in_specs=in_specs, out_specs=P(SEQ, "head"), check_vma=False
    )
```

```python
import jax
import jax.numpy as jnp
from jax import lax
from jax.experimental import pallas as pl
from jax.experimental.pallas import tpu as pltpu
from jax.sharding import Mesh
from jax.sharding import PartitionSpec as P

VD = 1280
VH = 16
HD = 128
FPATCH = 256
WIN = 64
SEQ = ("seq_0", "seq_1", "seq_2")
NZ, NY, NC, NX = 16, 4, 2, 4
ROWS = VD // (NZ * NY * NC)
PACKED = 24
COLS = VD // NX
HEAD = VD // VH
HEADS = COLS // HEAD
UNITS = FPATCH // 4
GROUP = 8
LAYER = NY * NC
NEGATIVE = -1e30
f32 = jnp.float32
bf16 = jnp.bfloat16


def dot(a, b):
    return lax.dot_general(a, b, (((1,), (0,)), ((), ())), preferred_element_type=f32)


def dot_t(a, b):
    return lax.dot_general(a, b, (((1,), (1,)), ((), ())), preferred_element_type=f32)


def iota(shape, dim):
    return lax.broadcasted_iota(jnp.int32, shape, dim)


def one_hot(condition):
    return jnp.where(condition, 1.0, 0.0).astype(bf16)


def copies_over(value, axes, count):
    copies = jnp.broadcast_to(value[None], (count, *value.shape))
    return lax.all_to_all(copies, axes, split_axis=0, concat_axis=0, tiled=True)


def call(body, outs, operands, specs=None, vmem=40 << 20):
    vm = pl.BlockSpec(memory_space=pltpu.VMEM)
    return pl.pallas_call(
        body,
        out_shape=outs,
        in_specs=specs or [vm] * len(operands),
        out_specs=jax.tree.map(lambda _: vm, outs),
        compiler_params=pltpu.CompilerParams(vmem_limit_bytes=vmem),
    )(*operands)


VMEM = pl.BlockSpec(memory_space=pltpu.VMEM)
SMEM = pl.BlockSpec(memory_space=pltpu.SMEM)


def prepare_kernel(
    length_ref, place_ref, patches_ref, gain_ref, merge_gain_ref, window_ref, asking_ref, suffix_ref,
    normed_ref, source_ref, merge_ref, order_ref, member_ref, mixed_ref, level_ref,
):
    shape = (VD, VD)
    row = iota((VD, 1), 0)
    z, y, c, r = row // (VD // NZ), row // (NC * ROWS) % NY, row // ROWS % NC, row % ROWS
    target = ((c + place_ref[2]) % NC) * (VD // NC) + (y * NZ + z) * ROWS + r
    order = one_hot(iota(shape, 1) == target)
    order_ref[...] = order
    source = patches_ref[...].astype(f32)
    scale = lax.rsqrt(jnp.mean(source * source, axis=-1, keepdims=True) + 1e-06)
    normed = (source * scale * gain_ref[...]).astype(bf16)
    normed_ref[...] = dot(normed, order).astype(bf16)
    shape = (UNITS, FPATCH)
    pick = one_hot(iota(shape, 1) == iota(shape, 0) * 4 + place_ref[3])
    source_ref[...] = dot(dot(pick, patches_ref[...]).astype(bf16), order)
    gain = merge_gain_ref[...]
    high = gain.astype(bf16).astype(f32)
    middle = (gain - high).astype(bf16).astype(f32)
    low = gain - high - middle
    part = iota((8, 1), 0)
    parts = jnp.where(part == 0, high, jnp.where(part == 1, middle, jnp.where(part == 2, low, 0.0)))
    merge_ref[...] = jnp.sum(dot(parts.astype(bf16), order), axis=0, keepdims=True)
    member = one_hot(window_ref[...] == iota((FPATCH, UNITS), 0) // 4)
    shape = (UNITS, 128)
    member_ref[...] = dot(member, one_hot(iota(shape, 0) // (WIN // 4) == iota(shape, 1))).astype(bf16)

    asking = asking_ref[...]
    count = asking.shape[0]
    span = suffix_ref.shape[0] // 2
    row = iota((count, 1), 0)
    even = (row // GROUP) % 2 == 0
    second = row // (2 * GROUP)
    scores = jnp.where(even, dot_t(asking, suffix_ref[:, 0:128]), dot_t(asking, suffix_ref[:, 128:256]))
    col = iota((1, 2 * span), 1)
    length = jnp.where(second == 0, length_ref[0], length_ref[1])
    live = (col // span == second) & (col % span < length)
    scores = jnp.where(live, scores * HD ** (-0.5), NEGATIVE)
    highest = jnp.max(scores, axis=-1, keepdims=True)
    weights = jnp.exp(scores - highest)
    total = jnp.sum(weights, axis=-1, keepdims=True)
    weights = weights.astype(bf16)
    mixed_ref[...] = jnp.where(even, dot(weights, suffix_ref[:, 256:384]), dot(weights, suffix_ref[:, 384:512]))
    lane = iota((1, HD), 1)
    level_ref[...] = jnp.where(lane == 0, highest, total)


def compact_kernel(got_ref, weights_ref):
    got = got_ref[...]
    shape = (NZ * ROWS, NZ * PACKED)
    row, col = iota(shape, 0), iota(shape, 1)
    for half in range(2):
        pick = one_hot(col == (row // ROWS) * PACKED + half * ROWS + row % ROWS)
        weights = dot(pick, got).astype(bf16)
        for k in range(NY):
            weights_ref[k, :, half * 640 : (half + 1) * 640] = weights


def vision_kernel(normed_ref, own_ref, other_ref, member_ref, out_ref):
    wide = 1024
    half = VD // 2
    projected = dot(normed_ref[:, :half], own_ref[:, :wide]) + dot(normed_ref[:, half:], other_ref[:, :wide])
    projected = projected.astype(bf16).astype(f32)
    query = pltpu.roll(projected[:, 0:384], 64, 1)
    key = projected[:, 256:640].astype(bf16)
    value = projected[:, 640:1024]
    together = dot_t(member_ref[...], member_ref[...]) > 0.5
    lane = iota((1, 384), 1)
    mixed = jnp.zeros((FPATCH, 384), f32)
    for h in range(HEADS):
        at = 64 + h * HEAD
        asking = jnp.where((lane >= at) & (lane < at + HEAD), query, 0.0).astype(bf16)
        scores = dot_t(asking, key) * HEAD ** (-0.5)
        scores = jnp.where(together, scores, NEGATIVE)
        weights = jnp.exp(scores - jnp.max(scores, axis=-1, keepdims=True))
        weights = (weights / jnp.sum(weights, axis=-1, keepdims=True)).astype(bf16)
        at = h * HEAD
        mixed += dot(weights, jnp.where((lane >= at) & (lane < at + HEAD), value, 0.0).astype(bf16))
    mixed = pltpu.roll(mixed, 64, 1).astype(bf16)
    shape = (FPATCH, FPATCH)
    row, col = iota(shape, 0), iota(shape, 1)
    mixed = dot(one_hot(col == (row % UNITS) * 4 + row // UNITS), mixed).astype(bf16)
    out_ref[:, :half] = dot_t(mixed, own_ref[:, 896:1280]).astype(bf16)
    out_ref[:, half:] = dot_t(mixed, other_ref[:, 896:1280]).astype(bf16)


def merge_kernel(got_ref, source_ref, gain_ref, order_ref, out_ref):
    hidden = source_ref[...]
    for k in range(NX):
        hidden += got_ref[k * UNITS : (k + 1) * UNITS].astype(f32)
    scale = lax.rsqrt(jnp.mean(hidden * hidden, axis=-1, keepdims=True) + 1e-06)
    merged = (hidden * scale * gain_ref[...]).astype(bf16)
    out_ref[...] = dot_t(merged, order_ref[...]).astype(bf16)


def visual_kernel(merged_ref, weights_ref, out_ref, held_ref, sems):
    rows = 4 * VD // NZ

    def copy(k):
        return pltpu.make_async_copy(
            weights_ref.at[k, pl.ds(0, rows)], held_ref.at[pl.ds(k * rows, rows)], sems.at[k]
        )

    for k in range(NZ):
        copy(k).start()
    total = jnp.zeros((UNITS, 512), f32)
    for i in range(4):
        for k in range(4):
            copy(i * 4 + k).wait()
        total += dot(merged_ref[i * UNITS : (i + 1) * UNITS], held_ref[i * VD : (i + 1) * VD])
    visual = total.astype(bf16)
    for k in range(LAYER):
        out_ref[k] = visual


def attend_kernel(place_ref, visual_ref, asked_ref, range_ref, out_ref):
    layer, inner = place_ref[0], place_ref[1]
    count = NZ * 4 * GROUP
    tokens = LAYER * UNITS
    asked = asked_ref[...]
    asking = jnp.concatenate([asked[:, b * HD : (b + 1) * HD] for b in range(4)], axis=0)
    row = iota((count, 1), 0)
    even = row % 4 < 2
    question = ((row // 8) % NZ * LAYER + inner) * 2 + (row // 4) % 2
    pick = one_hot(iota((count, 256), 1) == question)
    bounds = dot(pick, range_ref[...].astype(f32).astype(bf16))
    lower, upper = bounds[:, 0:1], bounds[:, 1:2]
    frame = (layer * LAYER + iota((1, tokens), 1) // UNITS).astype(f32)
    live = (frame >= lower) & (frame < upper)
    scores = jnp.where(even, dot_t(asking, visual_ref[:, 0:128]), dot_t(asking, visual_ref[:, 128:256]))
    scores = jnp.where(live, scores * HD ** (-0.5), NEGATIVE)
    highest = jnp.max(scores, axis=-1, keepdims=True)
    weights = jnp.exp(scores - highest)
    total = jnp.sum(weights, axis=-1, keepdims=True)
    weights = weights.astype(bf16)
    mixed = jnp.where(even, dot(weights, visual_ref[:, 256:384]), dot(weights, visual_ref[:, 384:512]))
    mixed = mixed / total
    level = highest + jnp.log(total)
    high = level.astype(bf16).astype(f32)
    middle = (level - high).astype(bf16).astype(f32)
    low = level - high - middle
    lane = iota((1, HD), 1)
    levels = jnp.where(lane == 0, high, jnp.where(lane == 1, middle, jnp.where(lane == 2, low, 0.0)))
    sent = jnp.concatenate([mixed, levels], axis=1).astype(bf16)
    shape = (count, count)
    row, col = iota(shape, 0), iota(shape, 1)
    head = row % 16
    order = one_hot(col == (head % 4) * (NZ * 8) + row // 32 * 8 + row // 16 % 2 * 4 + head // 4)
    out_ref[...] = dot(order, sent).astype(bf16)


def answer_kernel(got_ref, mixed_ref, level_ref, out_ref):
    count = mixed_ref.shape[0]
    highest, total = level_ref[:, 0:1], level_ref[:, 1:2]
    levels = []
    top = highest
    for k in range(NZ):
        parts = got_ref[k * count : (k + 1) * count, HD:].astype(f32)
        level = parts[:, 0:1] + parts[:, 1:2] + parts[:, 2:3]
        levels.append(level)
        top = jnp.maximum(top, level)
    share = jnp.exp(highest - top)
    mixed = mixed_ref[...] * share
    total = total * share
    for k in range(NZ):
        share = jnp.exp(levels[k] - top)
        mixed += got_ref[k * count : (k + 1) * count, :HD].astype(f32) * share
        total += share
    mixed = mixed / total
    heads = count // 2
    for h in range(heads):
        pair = jnp.concatenate([mixed[h : h + 1], mixed[heads + h : heads + h + 1]], axis=0)
        out_ref[:, h * HD : (h + 1) * HD] = pair.astype(bf16)


def on_device(
    patches,
    norm_gain,
    w_qkv,
    w_out,
    window_order,
    merge_gain,
    w_kv,
    queries,
    suffix_kv,
    question_lengths,
    frame_range,
):
    sds = jax.ShapeDtypeStruct
    barrier = lax.optimization_barrier
    layer = lax.axis_index("seq_0")
    inner = lax.axis_index(("seq_1", "seq_2"))
    place = jnp.stack([layer, inner, lax.axis_index("seq_2"), lax.axis_index("head")])

    near = copies_over(w_kv.reshape(-1, 512), ("seq_1", "seq_2"), LAYER).reshape(-1, 512)
    packed = jnp.concatenate([w_qkv.reshape(ROWS, 3 * COLS), w_out.T], axis=1)
    packed = jnp.concatenate(
        [packed[:, :640], packed[:, 640:], jnp.zeros((PACKED - 2 * ROWS, 640), bf16)], axis=0
    )
    packed, near = barrier((packed, near))
    asked = jnp.concatenate([queries.reshape(8, 512), jnp.zeros((8, 512), bf16)], axis=0)
    near = jnp.concatenate([near, asked], axis=0)
    far = lax.all_gather(near, "seq_0", axis=0)

    prepared = call(
        prepare_kernel,
        (
            sds((FPATCH, VD), bf16),
            sds((UNITS, VD), f32),
            sds((1, VD), f32),
            sds((VD, VD), bf16),
            sds((FPATCH, 128), bf16),
            sds((4 * GROUP, HD), f32),
            sds((4 * GROUP, HD), f32),
        ),
        (
            question_lengths, place, patches, norm_gain.reshape(1, VD), merge_gain.reshape(1, VD),
            window_order, queries.reshape(4 * GROUP, HD), suffix_kv.reshape(-1, 512),
        ),
        [SMEM] * 2 + [VMEM] * 6,
    )
    got = copies_over(packed, "seq_0", NZ).reshape(NZ * PACKED, 640)
    got, prepared, place, ranges = barrier((got, prepared, place, frame_range))
    normed, source, merge, order, member, mixed, level = prepared
    weights = call(compact_kernel, sds((NY, NZ * ROWS, VD), bf16), (got,))
    own = lax.all_to_all(weights, "seq_1", split_axis=0, concat_axis=0, tiled=True).reshape(VD // 2, VD)
    other = lax.ppermute(own, "seq_2", [(0, 1), (1, 0)])
    partial = call(vision_kernel, sds((FPATCH, VD), bf16), (normed, own, other, member))
    partial = lax.all_to_all(
        partial.reshape(NX, UNITS, VD), "head", split_axis=0, concat_axis=0, tiled=True
    ).reshape(FPATCH, VD)
    merged = call(merge_kernel, sds((UNITS, VD), bf16), (partial, source, merge, order))
    merged = lax.all_gather(merged, "head", axis=0, tiled=True)
    visual = pl.pallas_call(
        visual_kernel,
        out_shape=sds((LAYER, UNITS, 512), bf16),
        in_specs=[VMEM, pl.BlockSpec(memory_space=pltpu.HBM)],
        out_specs=VMEM,
        scratch_shapes=[pltpu.VMEM((4 * VD, 512), bf16), pltpu.SemaphoreType.DMA((NZ,))],
        compiler_params=pltpu.CompilerParams(vmem_limit_bytes=40 << 20),
    )(merged, far)
    asked = far[:, -16:-8].reshape(NZ * 8, 512)
    visual = lax.all_to_all(
        visual, ("seq_1", "seq_2"), split_axis=0, concat_axis=0, tiled=True
    ).reshape(LAYER * UNITS, 512)
    sent = call(
        attend_kernel,
        sds((NZ * 4 * GROUP, 2 * HD), bf16),
        (place, visual, asked, ranges),
        [SMEM] + [VMEM] * 3,
    )
    got = lax.all_to_all(
        sent.reshape(NZ, 4 * GROUP, 2 * HD), "seq_0", split_axis=0, concat_axis=0, tiled=True
    ).reshape(-1, 2 * HD)
    return call(answer_kernel, sds((2, 2 * GROUP * HD), bf16), (got, mixed, level))


def solution(mesh):
    torus = Mesh(
        mesh.devices.reshape(NZ, NY, NC, NX), ("seq_0", "seq_1", "seq_2", "head")
    )
    in_specs = (
        P(SEQ, None),
        P(),
        P(SEQ, None, "head"),
        P("head", SEQ),
        P(SEQ, None),
        P(),
        P(SEQ, None, "head"),
        P(SEQ, "head"),
        P(SEQ, None, None, "head"),
        P(SEQ),
        P(),
    )
    return jax.shard_map(
        on_device, mesh=torus, in_specs=in_specs, out_specs=P(SEQ, "head"), check_vma=False
    )
```

```python
import jax
import jax.numpy as jnp
from jax import lax
from jax.experimental import pallas as pl
from jax.experimental.pallas import tpu as pltpu
from jax.sharding import Mesh
from jax.sharding import PartitionSpec as P

VD = 1280
VH = 16
HD = 128
FPATCH = 256
WIN = 64
SEQ = ("seq_0", "seq_1", "seq_2")
NZ, NY, NC, NX = 16, 4, 2, 4
ROWS = VD // (NZ * NY * NC)
PACKED = 24
SENT = 40
COLS = VD // NX
HEAD = VD // VH
HEADS = COLS // HEAD
UNITS = FPATCH // 4
GROUP = 8
LAYER = NY * NC
NEGATIVE = -1e30
f32 = jnp.float32
bf16 = jnp.bfloat16


def dot(a, b):
    return lax.dot_general(a, b, (((1,), (0,)), ((), ())), preferred_element_type=f32)


def dot_t(a, b):
    return lax.dot_general(a, b, (((1,), (1,)), ((), ())), preferred_element_type=f32)


def iota(shape, dim):
    return lax.broadcasted_iota(jnp.int32, shape, dim)


def one_hot(condition):
    return jnp.where(condition, 1.0, 0.0).astype(bf16)


def copies_over(value, axes, count):
    copies = jnp.broadcast_to(value[None], (count, *value.shape))
    return lax.all_to_all(copies, axes, split_axis=0, concat_axis=0, tiled=True)


def call(body, outs, operands, specs=None, vmem=24 << 20):
    vm = pl.BlockSpec(memory_space=pltpu.VMEM)
    return pl.pallas_call(
        body,
        out_shape=outs,
        in_specs=specs or [vm] * len(operands),
        out_specs=jax.tree.map(lambda _: vm, outs),
        compiler_params=pltpu.CompilerParams(vmem_limit_bytes=vmem),
    )(*operands)


VMEM = pl.BlockSpec(memory_space=pltpu.VMEM)
SMEM = pl.BlockSpec(memory_space=pltpu.SMEM)


def prepare_kernel(
    length_ref, place_ref, patches_ref, gain_ref, merge_gain_ref, window_ref, asking_ref, suffix_ref,
    normed_ref, source_ref, merge_ref, turn_ref, member_ref, mixed_ref, level_ref,
):
    shape = (VD, VD)
    core, inner = place_ref[2], place_ref[1]
    row = iota((VD, 1), 0)
    z, y, c, r = row // (VD // NZ), row // (NC * ROWS) % NY, row // ROWS % NC, row % ROWS
    target = ((c + core) % NC) * (VD // NC) + (y * NZ + z) * ROWS + r
    order = one_hot(iota(shape, 1) == target)
    half, y, z, r = row // (VD // NC), row // (NZ * ROWS) % NY, row // ROWS % NZ, row % ROWS
    natural = ((z * NY + y) * NC + (half + core) % NC) * ROWS + r
    deep = 4 * ROWS
    z, y, c, r = natural // (LAYER * deep), natural // (NC * deep) % NY, natural // deep % NC, natural % deep
    away = (inner // NC - y + NY) % NY
    target = ((c + core) % NC) * (VD // NC) + (z * NY + away) * deep + r
    turn_ref[...] = one_hot(iota(shape, 1) == target)
    source = patches_ref[...].astype(f32)
    scale = lax.rsqrt(jnp.mean(source * source, axis=-1, keepdims=True) + 1e-06)
    normed = (source * scale * gain_ref[...]).astype(bf16)
    normed_ref[...] = dot(normed, order).astype(bf16)
    shape = (UNITS, FPATCH)
    pick = one_hot(iota(shape, 1) == iota(shape, 0) * 4 + place_ref[3])
    source_ref[...] = dot(dot(pick, patches_ref[...]).astype(bf16), order)
    gain = merge_gain_ref[...]
    high = gain.astype(bf16).astype(f32)
    middle = (gain - high).astype(bf16).astype(f32)
    low = gain - high - middle
    part = iota((8, 1), 0)
    parts = jnp.where(part == 0, high, jnp.where(part == 1, middle, jnp.where(part == 2, low, 0.0)))
    merge_ref[...] = jnp.sum(dot(parts.astype(bf16), order), axis=0, keepdims=True)
    member = one_hot(window_ref[...] == iota((FPATCH, UNITS), 0) // 4)
    shape = (UNITS, 128)
    member_ref[...] = dot(member, one_hot(iota(shape, 0) // (WIN // 4) == iota(shape, 1))).astype(bf16)

    asking = asking_ref[...]
    count = asking.shape[0]
    span = suffix_ref.shape[0] // 2
    row = iota((count, 1), 0)
    even = (row // GROUP) % 2 == 0
    second = row // (2 * GROUP)
    scores = jnp.where(even, dot_t(asking, suffix_ref[:, 0:128]), dot_t(asking, suffix_ref[:, 128:256]))
    col = iota((1, 2 * span), 1)
    length = jnp.where(second == 0, length_ref[0], length_ref[1])
    live = (col // span == second) & (col % span < length)
    scores = jnp.where(live, scores * HD ** (-0.5), NEGATIVE)
    highest = jnp.max(scores, axis=-1, keepdims=True)
    weights = jnp.exp(scores - highest)
    total = jnp.sum(weights, axis=-1, keepdims=True)
    weights = weights.astype(bf16)
    mixed_ref[...] = jnp.where(even, dot(weights, suffix_ref[:, 256:384]), dot(weights, suffix_ref[:, 384:512]))
    lane = iota((1, HD), 1)
    level_ref[...] = jnp.where(lane == 0, highest, total)


def compact_kernel(got_ref, weights_ref):
    got = got_ref[...]
    shape = (NZ * ROWS, NZ * PACKED)
    row, col = iota(shape, 0), iota(shape, 1)
    for half in range(2):
        pick = one_hot(col == (row // ROWS) * PACKED + half * ROWS + row % ROWS)
        weights = dot(pick, got).astype(bf16)
        for k in range(NY):
            weights_ref[k, :, half * 640 : (half + 1) * 640] = weights


def vision_kernel(normed_ref, own_ref, other_ref, member_ref, out_ref):
    wide = 1024
    half = VD // 2
    projected = dot(normed_ref[:, :half], own_ref[:, :wide]) + dot(normed_ref[:, half:], other_ref[:, :wide])
    projected = projected.astype(bf16).astype(f32)
    query = pltpu.roll(projected[:, 0:384], 64, 1)
    key = projected[:, 256:640].astype(bf16)
    value = projected[:, 640:1024]
    together = dot_t(member_ref[...], member_ref[...]) > 0.5
    lane = iota((1, 384), 1)
    mixed = jnp.zeros((FPATCH, 384), f32)
    for h in range(HEADS):
        at = 64 + h * HEAD
        asking = jnp.where((lane >= at) & (lane < at + HEAD), query, 0.0).astype(bf16)
        scores = dot_t(asking, key) * HEAD ** (-0.5)
        scores = jnp.where(together, scores, NEGATIVE)
        weights = jnp.exp(scores - jnp.max(scores, axis=-1, keepdims=True))
        weights = (weights / jnp.sum(weights, axis=-1, keepdims=True)).astype(bf16)
        at = h * HEAD
        mixed += dot(weights, jnp.where((lane >= at) & (lane < at + HEAD), value, 0.0).astype(bf16))
    mixed = pltpu.roll(mixed, 64, 1).astype(bf16)
    shape = (FPATCH, FPATCH)
    row, col = iota(shape, 0), iota(shape, 1)
    mixed = dot(one_hot(col == (row % UNITS) * 4 + row // UNITS), mixed).astype(bf16)
    out_ref[:, :half] = dot_t(mixed, own_ref[:, 896:1280]).astype(bf16)
    out_ref[:, half:] = dot_t(mixed, other_ref[:, 896:1280]).astype(bf16)


def merge_kernel(got_ref, source_ref, gain_ref, turn_ref, out_ref):
    hidden = source_ref[...]
    for k in range(NX):
        hidden += got_ref[k * UNITS : (k + 1) * UNITS].astype(f32)
    scale = lax.rsqrt(jnp.mean(hidden * hidden, axis=-1, keepdims=True) + 1e-06)
    merged = (hidden * scale * gain_ref[...]).astype(bf16)
    out_ref[...] = dot(merged, turn_ref[...]).astype(bf16)


def visual_kernel(merged_ref, own_ref, other_ref, out_ref):
    rows = 4 * NY * ROWS
    half = VD // 2
    total = jnp.zeros((UNITS, 512), f32)
    for i in range(4):
        merged = merged_ref[i * UNITS : (i + 1) * UNITS]
        for part, ref in ((merged[:, :half], own_ref), (merged[:, half:], other_ref)):
            weights = jnp.concatenate([ref[i * 4 + k, :rows] for k in range(4)], axis=0)
            total += dot(part, weights)
    visual = total.astype(bf16)
    for k in range(LAYER):
        out_ref[k] = visual


def attend_kernel(place_ref, visual_ref, asked_ref, range_ref, out_ref):
    layer, inner = place_ref[0], place_ref[1]
    count = NZ * 4 * GROUP
    tokens = LAYER * UNITS
    asked = asked_ref[...]
    asking = jnp.concatenate([asked[:, b * HD : (b + 1) * HD] for b in range(4)], axis=0)
    row = iota((count, 1), 0)
    even = row % 4 < 2
    question = ((row // 8) % NZ * LAYER + inner) * 2 + (row // 4) % 2
    pick = one_hot(iota((count, 256), 1) == question)
    bounds = dot(pick, range_ref[...].astype(f32).astype(bf16))
    lower, upper = bounds[:, 0:1], bounds[:, 1:2]
    frame = (layer * LAYER + iota((1, tokens), 1) // UNITS).astype(f32)
    live = (frame >= lower) & (frame < upper)
    scores = jnp.where(even, dot_t(asking, visual_ref[:, 0:128]), dot_t(asking, visual_ref[:, 128:256]))
    scores = jnp.where(live, scores * HD ** (-0.5), NEGATIVE)
    highest = jnp.max(scores, axis=-1, keepdims=True)
    weights = jnp.exp(scores - highest)
    total = jnp.sum(weights, axis=-1, keepdims=True)
    weights = weights.astype(bf16)
    mixed = jnp.where(even, dot(weights, visual_ref[:, 256:384]), dot(weights, visual_ref[:, 384:512]))
    mixed = mixed / total
    level = highest + jnp.log(total)
    high = level.astype(bf16).astype(f32)
    middle = (level - high).astype(bf16).astype(f32)
    low = level - high - middle
    lane = iota((1, HD), 1)
    place = row // 4 % 2 * 16 + row % 4 * 4 + row // (NZ * 8)
    levels = jnp.where(
        lane == place,
        high,
        jnp.where(lane == place + 32, middle, jnp.where(lane == place + 64, low, 0.0)),
    )
    shape = (NZ * SENT, count)
    row, col = iota((NZ * SENT, 1), 0), iota(shape, 1)
    z, at = row // SENT, row % SENT
    head = at % 16
    source = jnp.where(at < 32, (head % 4) * (NZ * 8) + z * 8 + at // 16 * 4 + head // 4, -1)
    order = one_hot(col == source)
    layers = one_hot(iota((1, count), 1) // 8 % NZ == jnp.where(at == 32, z, -1))
    out_ref[...] = (dot(order, mixed.astype(bf16)) + dot(layers, levels.astype(bf16))).astype(bf16)


def answer_kernel(got_ref, mixed_ref, level_ref, out_ref):
    count = mixed_ref.shape[0]
    highest, total = level_ref[:, 0:1], level_ref[:, 1:2]
    got = got_ref[...].astype(f32)
    shape = (count, HD)
    mine = iota(shape, 1) % count == iota(shape, 0)
    levels = []
    top = highest
    for k in range(NZ):
        row = got[k * SENT + count : k * SENT + count + 1]
        level = jnp.sum(jnp.where(mine, row, 0.0), axis=-1, keepdims=True)
        levels.append(level)
        top = jnp.maximum(top, level)
    share = jnp.exp(highest - top)
    mixed = mixed_ref[...] * share
    total = total * share
    for k in range(NZ):
        share = jnp.exp(levels[k] - top)
        mixed += got[k * SENT : k * SENT + count] * share
        total += share
    mixed = mixed / total
    heads = count // 2
    for h in range(heads):
        pair = jnp.concatenate([mixed[h : h + 1], mixed[heads + h : heads + h + 1]], axis=0)
        out_ref[:, h * HD : (h + 1) * HD] = pair.astype(bf16)


def on_device(
    patches,
    norm_gain,
    w_qkv,
    w_out,
    window_order,
    merge_gain,
    w_kv,
    queries,
    suffix_kv,
    question_lengths,
    frame_range,
):
    sds = jax.ShapeDtypeStruct
    barrier = lax.optimization_barrier
    layer = lax.axis_index("seq_0")
    inner = lax.axis_index(("seq_1", "seq_2"))
    place = jnp.stack([layer, inner, lax.axis_index("seq_2"), lax.axis_index("head")])

    near = [w_kv.reshape(-1, 512)]
    for away in range(1, NY):
        near.append(lax.ppermute(near[0], "seq_1", [(k, (k + away) % NY) for k in range(NY)]))
    packed = jnp.concatenate([w_qkv.reshape(ROWS, 3 * COLS), w_out.T], axis=1)
    packed = jnp.concatenate(
        [packed[:, :640], packed[:, 640:], jnp.zeros((PACKED - 2 * ROWS, 640), bf16)], axis=0
    )
    near = jnp.concatenate([*near, queries.reshape(8, 512), jnp.zeros((8, 512), bf16)], axis=0)
    far = lax.all_gather(near, "seq_0", axis=0)

    prepared = call(
        prepare_kernel,
        (
            sds((FPATCH, VD), bf16),
            sds((UNITS, VD), f32),
            sds((1, VD), f32),
            sds((VD, VD), bf16),
            sds((FPATCH, 128), bf16),
            sds((4 * GROUP, HD), f32),
            sds((4 * GROUP, HD), f32),
        ),
        (
            question_lengths, place, patches, norm_gain.reshape(1, VD), merge_gain.reshape(1, VD),
            window_order, queries.reshape(4 * GROUP, HD), suffix_kv.reshape(-1, 512),
        ),
        [SMEM] * 2 + [VMEM] * 6,
    )
    got = copies_over(packed, "seq_0", NZ).reshape(NZ * PACKED, 640)
    got, prepared, place, ranges = barrier((got, prepared, place, frame_range))
    normed, source, merge, turn, member, mixed, level = prepared
    weights = call(compact_kernel, sds((NY, NZ * ROWS, VD), bf16), (got,))
    own = lax.all_to_all(weights, "seq_1", split_axis=0, concat_axis=0, tiled=True).reshape(VD // 2, VD)
    other = lax.ppermute(own, "seq_2", [(0, 1), (1, 0)])
    partial = call(vision_kernel, sds((FPATCH, VD), bf16), (normed, own, other, member))
    partial = lax.all_to_all(
        partial.reshape(NX, UNITS, VD), "head", split_axis=0, concat_axis=0, tiled=True
    ).reshape(FPATCH, VD)
    partial, far = barrier((partial, far))
    far_other = lax.ppermute(far, "seq_2", [(0, 1), (1, 0)])
    merged = call(merge_kernel, sds((UNITS, VD), bf16), (partial, source, merge, turn))
    merged = lax.all_gather(merged, "head", axis=0, tiled=True)
    visual = call(visual_kernel, sds((LAYER, UNITS, 512), bf16), (merged, far, far_other), vmem=24 << 20)
    asked = far[:, -16:-8].reshape(NZ * 8, 512)
    visual = lax.all_to_all(
        visual, ("seq_1", "seq_2"), split_axis=0, concat_axis=0, tiled=True
    ).reshape(LAYER * UNITS, 512)
    sent = call(
        attend_kernel,
        sds((NZ * SENT, HD), bf16),
        (place, visual, asked, ranges),
        [SMEM] + [VMEM] * 3,
    )
    got = lax.all_to_all(
        sent.reshape(NZ, SENT, HD), "seq_0", split_axis=0, concat_axis=0, tiled=True
    ).reshape(-1, HD)
    return call(answer_kernel, sds((2, 2 * GROUP * HD), bf16), (got, mixed, level))


def solution(mesh):
    torus = Mesh(
        mesh.devices.reshape(NZ, NY, NC, NX), ("seq_0", "seq_1", "seq_2", "head")
    )
    in_specs = (
        P(SEQ, None),
        P(),
        P(SEQ, None, "head"),
        P("head", SEQ),
        P(SEQ, None),
        P(),
        P(SEQ, None, "head"),
        P(SEQ, "head"),
        P(SEQ, None, None, "head"),
        P(SEQ),
        P(),
    )
    return jax.shard_map(
        on_device, mesh=torus, in_specs=in_specs, out_specs=P(SEQ, "head"), check_vma=False
    )
```

```python
import jax
import jax.numpy as jnp
from jax import lax
from jax.experimental import pallas as pl
from jax.experimental.pallas import tpu as pltpu
from jax.sharding import Mesh
from jax.sharding import PartitionSpec as P

VD = 1280
VH = 16
HD = 128
FPATCH = 256
WIN = 64
SEQ = ("seq_0", "seq_1", "seq_2")
NZ, NY, NC, NX = 16, 4, 2, 4
ROWS = VD // (NZ * NY * NC)
PACKED = 24
SENT = 40
COLS = VD // NX
HEAD = VD // VH
HEADS = COLS // HEAD
UNITS = FPATCH // 4
GROUP = 8
LAYER = NY * NC
NEGATIVE = -1e30
f32 = jnp.float32
bf16 = jnp.bfloat16


def dot(a, b):
    return lax.dot_general(a, b, (((1,), (0,)), ((), ())), preferred_element_type=f32)


def dot_t(a, b):
    return lax.dot_general(a, b, (((1,), (1,)), ((), ())), preferred_element_type=f32)


def iota(shape, dim):
    return lax.broadcasted_iota(jnp.int32, shape, dim)


def one_hot(condition):
    return jnp.where(condition, 1.0, 0.0).astype(bf16)


def copies_over(value, axes, count):
    copies = jnp.broadcast_to(value[None], (count, *value.shape))
    return lax.all_to_all(copies, axes, split_axis=0, concat_axis=0, tiled=True)


def call(body, outs, operands, specs=None, vmem=24 << 20):
    vm = pl.BlockSpec(memory_space=pltpu.VMEM)
    return pl.pallas_call(
        body,
        out_shape=outs,
        in_specs=specs or [vm] * len(operands),
        out_specs=jax.tree.map(lambda _: vm, outs),
        compiler_params=pltpu.CompilerParams(vmem_limit_bytes=vmem),
    )(*operands)


VMEM = pl.BlockSpec(memory_space=pltpu.VMEM)
SMEM = pl.BlockSpec(memory_space=pltpu.SMEM)


def places():
    at = iota((VD, 1), 0)
    return at // (NY * NC * ROWS), at // (NC * ROWS) % NY, at // ROWS % NC, at % ROWS


def prepare_kernel(place_ref, patches_ref, gain_ref, window_ref, normed_ref, member_ref):
    core = place_ref[2]
    z, y, c, r = places()
    target = ((c + core) % NC) * (VD // NC) + (y * NZ + z) * ROWS + r
    order = one_hot(iota((VD, VD), 1) == target)
    source = patches_ref[...].astype(f32)
    scale = lax.rsqrt(jnp.mean(source * source, axis=-1, keepdims=True) + 1e-06)
    normed = (source * scale * gain_ref[...]).astype(bf16)
    normed_ref[...] = dot(normed, order).astype(bf16)
    member = one_hot(window_ref[...] == iota((FPATCH, UNITS), 0) // 4)
    shape = (UNITS, 128)
    member_ref[...] = dot(member, one_hot(iota(shape, 0) // (WIN // 4) == iota(shape, 1))).astype(bf16)


def residual_kernel(place_ref, patches_ref, gain_ref, source_ref, gains_ref, turn_ref):
    core = place_ref[2]
    z, y, c, r = places()
    target = ((y // 2 + core) % NC) * (VD // NC) + ((c * 2 + y % 2) * NZ + z) * ROWS + r
    order = one_hot(iota((VD, VD), 1) == target)
    shape = (UNITS, FPATCH)
    pick = one_hot(iota(shape, 1) == iota(shape, 0) * 4 + place_ref[3])
    source_ref[...] = dot(dot(pick, patches_ref[...]).astype(bf16), order)
    gain = gain_ref[...]
    high = gain.astype(bf16).astype(f32)
    middle = (gain - high).astype(bf16).astype(f32)
    low = gain - high - middle
    part = iota((8, 1), 0)
    parts = jnp.where(part == 0, high, jnp.where(part == 1, middle, jnp.where(part == 2, low, 0.0)))
    gains_ref[...] = jnp.sum(dot(parts.astype(bf16), order), axis=0, keepdims=True)
    half = VD // 2
    row = iota((half, 1), 0)
    c, y, z, r = row // (2 * NZ * ROWS), row // (NZ * ROWS) % 2, row // ROWS % NZ, row % ROWS
    turn_ref[...] = one_hot(iota((half, half), 1) == ((z * 2 + y) * NC + c) * ROWS + r)


def suffix_kernel(length_ref, asking_ref, suffix_ref, mixed_ref, level_ref):
    asking = asking_ref[...]
    count = asking.shape[0]
    span = suffix_ref.shape[0] // 2
    row = iota((count, 1), 0)
    even = (row // GROUP) % 2 == 0
    second = row // (2 * GROUP)
    scores = jnp.where(even, dot_t(asking, suffix_ref[:, 0:128]), dot_t(asking, suffix_ref[:, 128:256]))
    col = iota((1, 2 * span), 1)
    length = jnp.where(second == 0, length_ref[0], length_ref[1])
    live = (col // span == second) & (col % span < length)
    scores = jnp.where(live, scores * HD ** (-0.5), NEGATIVE)
    highest = jnp.max(scores, axis=-1, keepdims=True)
    weights = jnp.exp(scores - highest)
    total = jnp.sum(weights, axis=-1, keepdims=True)
    weights = weights.astype(bf16)
    mixed_ref[...] = jnp.where(even, dot(weights, suffix_ref[:, 256:384]), dot(weights, suffix_ref[:, 384:512]))
    level_ref[...] = jnp.where(iota((1, HD), 1) == 0, highest, total)


def compact_kernel(got_ref, weights_ref):
    got = got_ref[...]
    shape = (NZ * ROWS, NZ * PACKED)
    row, col = iota(shape, 0), iota(shape, 1)
    for half in range(2):
        pick = one_hot(col == (row // ROWS) * PACKED + half * ROWS + row % ROWS)
        weights = dot(pick, got).astype(bf16)
        for k in range(NY):
            weights_ref[k, :, half * 640 : (half + 1) * 640] = weights


def vision_kernel(place_ref, normed_ref, own_ref, other_ref, member_ref, out_ref):
    wide = 1024
    half = VD // 2
    projected = dot(normed_ref[:, :half], own_ref[:, :wide]) + dot(normed_ref[:, half:], other_ref[:, :wide])
    projected = projected.astype(bf16).astype(f32)
    query = pltpu.roll(projected[:, 0:384], 64, 1)
    key = projected[:, 256:640].astype(bf16)
    value = projected[:, 640:1024]
    together = dot_t(member_ref[...], member_ref[...]) > 0.5
    lane = iota((1, 384), 1)
    mixed = jnp.zeros((FPATCH, 384), f32)
    for h in range(HEADS):
        at = 64 + h * HEAD
        asking = jnp.where((lane >= at) & (lane < at + HEAD), query, 0.0).astype(bf16)
        scores = dot_t(asking, key) * HEAD ** (-0.5)
        scores = jnp.where(together, scores, NEGATIVE)
        weights = jnp.exp(scores - jnp.max(scores, axis=-1, keepdims=True))
        weights = (weights / jnp.sum(weights, axis=-1, keepdims=True)).astype(bf16)
        at = h * HEAD
        mixed += dot(weights, jnp.where((lane >= at) & (lane < at + HEAD), value, 0.0).astype(bf16))
    mixed = pltpu.roll(mixed, 64, 1).astype(bf16)
    shape = (FPATCH, FPATCH)
    row, col = iota(shape, 0), iota(shape, 1)
    mixed = dot(one_hot(col == (row % UNITS) * 4 + row // UNITS), mixed).astype(bf16)

    def project(core):
        pair = (own_ref, other_ref) if core == 0 else (other_ref, own_ref)
        for part in range(2):
            rows = slice((part ^ core) * half // 2, ((part ^ core) + 1) * half // 2)
            weights = jnp.concatenate([ref[rows, 896:1280] for ref in pair], axis=0)
            out_ref[:, part * half : (part + 1) * half] = dot_t(mixed, weights).astype(bf16)

    for core in range(NC):
        pl.when(place_ref[2] == core)(lambda core=core: project(core))


def merge_kernel(got_ref, source_ref, gain_ref, turn_ref, out_ref):
    hidden = source_ref[...]
    for k in range(NX):
        hidden += got_ref[k * UNITS : (k + 1) * UNITS].astype(f32)
    scale = lax.rsqrt(jnp.mean(hidden * hidden, axis=-1, keepdims=True) + 1e-06)
    merged = (hidden * scale * gain_ref[...]).astype(bf16)
    half = VD // 2
    for part in range(2):
        at = slice(part * half, (part + 1) * half)
        out_ref[:, at] = dot(merged[:, at], turn_ref[...]).astype(bf16)


def visual_kernel(merged_ref, own_ref, other_ref, out_ref):
    rows = 4 * NY * ROWS
    half = VD // 2
    total = jnp.zeros((UNITS, 512), f32)
    for i in range(4):
        merged = merged_ref[i * UNITS : (i + 1) * UNITS]
        for part, ref in ((merged[:, :half], own_ref), (merged[:, half:], other_ref)):
            weights = jnp.concatenate([ref[i * 4 + k, :rows] for k in range(4)], axis=0)
            total += dot(part, weights)
    visual = total.astype(bf16)
    for k in range(LAYER):
        out_ref[k] = visual


def attend_kernel(place_ref, visual_ref, asked_ref, range_ref, out_ref):
    layer, inner = place_ref[0], place_ref[1]
    count = NZ * 4 * GROUP
    tokens = LAYER * UNITS
    asked = asked_ref[...]
    asking = jnp.concatenate([asked[:, b * HD : (b + 1) * HD] for b in range(4)], axis=0)
    row = iota((count, 1), 0)
    even = row % 4 < 2
    question = ((row // 8) % NZ * LAYER + inner) * 2 + (row // 4) % 2
    pick = one_hot(iota((count, 256), 1) == question)
    bounds = dot(pick, range_ref[...].astype(f32).astype(bf16))
    lower, upper = bounds[:, 0:1], bounds[:, 1:2]
    frame = (layer * LAYER + iota((1, tokens), 1) // UNITS).astype(f32)
    live = (frame >= lower) & (frame < upper)
    scores = jnp.where(even, dot_t(asking, visual_ref[:, 0:128]), dot_t(asking, visual_ref[:, 128:256]))
    scores = jnp.where(live, scores * HD ** (-0.5), NEGATIVE)
    highest = jnp.max(scores, axis=-1, keepdims=True)
    weights = jnp.exp(scores - highest)
    total = jnp.sum(weights, axis=-1, keepdims=True)
    weights = weights.astype(bf16)
    mixed = jnp.where(even, dot(weights, visual_ref[:, 256:384]), dot(weights, visual_ref[:, 384:512]))
    mixed = mixed / total
    level = highest + jnp.log(total)
    high = level.astype(bf16).astype(f32)
    middle = (level - high).astype(bf16).astype(f32)
    low = level - high - middle
    lane = iota((1, HD), 1)
    place = row // 4 % 2 * 16 + row % 4 * 4 + row // (NZ * 8)
    levels = jnp.where(
        lane == place,
        high,
        jnp.where(lane == place + 32, middle, jnp.where(lane == place + 64, low, 0.0)),
    )
    shape = (NZ * SENT, count)
    row, col = iota((NZ * SENT, 1), 0), iota(shape, 1)
    z, at = row // SENT, row % SENT
    head = at % 16
    source = jnp.where(at < 32, (head % 4) * (NZ * 8) + z * 8 + at // 16 * 4 + head // 4, -1)
    order = one_hot(col == source)
    layers = one_hot(iota((1, count), 1) // 8 % NZ == jnp.where(at == 32, z, -1))
    out_ref[...] = (dot(order, mixed.astype(bf16)) + dot(layers, levels.astype(bf16))).astype(bf16)


def answer_kernel(got_ref, mixed_ref, level_ref, out_ref):
    count = mixed_ref.shape[0]
    highest, total = level_ref[:, 0:1], level_ref[:, 1:2]
    got = got_ref[...].astype(f32)
    shape = (count, HD)
    mine = iota(shape, 1) % count == iota(shape, 0)
    levels = []
    top = highest
    for k in range(NZ):
        row = got[k * SENT + count : k * SENT + count + 1]
        level = jnp.sum(jnp.where(mine, row, 0.0), axis=-1, keepdims=True)
        levels.append(level)
        top = jnp.maximum(top, level)
    share = jnp.exp(highest - top)
    mixed = mixed_ref[...] * share
    total = total * share
    for k in range(NZ):
        share = jnp.exp(levels[k] - top)
        mixed += got[k * SENT : k * SENT + count] * share
        total += share
    mixed = mixed / total
    heads = count // 2
    for h in range(heads):
        pair = jnp.concatenate([mixed[h : h + 1], mixed[heads + h : heads + h + 1]], axis=0)
        out_ref[:, h * HD : (h + 1) * HD] = pair.astype(bf16)


def on_device(
    patches,
    norm_gain,
    w_qkv,
    w_out,
    window_order,
    merge_gain,
    w_kv,
    queries,
    suffix_kv,
    question_lengths,
    frame_range,
):
    sds = jax.ShapeDtypeStruct
    barrier = lax.optimization_barrier
    layer = lax.axis_index("seq_0")
    inner = lax.axis_index(("seq_1", "seq_2"))
    place = jnp.stack([layer, inner, lax.axis_index("seq_2"), lax.axis_index("head")])

    near = copies_over(w_kv.reshape(-1, 512), "seq_1", NY).reshape(-1, 512)
    packed = jnp.concatenate([w_qkv.reshape(ROWS, 3 * COLS), w_out.T], axis=1)
    packed = jnp.concatenate(
        [packed[:, :640], packed[:, 640:], jnp.zeros((PACKED - 2 * ROWS, 640), bf16)], axis=0
    )
    packed, near = barrier((packed, near))
    near = jnp.concatenate([near, queries.reshape(8, 512), jnp.zeros((8, 512), bf16)], axis=0)
    far = lax.all_gather(near, "seq_0", axis=0)
    got = lax.all_gather(packed, "seq_0", axis=0, tiled=True)
    weights = call(compact_kernel, sds((NY, NZ * ROWS, VD), bf16), (got,))

    weights, patches, place, norm_gain, window_order = barrier((weights, patches, place, norm_gain, window_order))
    normed, member = call(
        prepare_kernel,
        (sds((FPATCH, VD), bf16), sds((FPATCH, 128), bf16)),
        (place, patches, norm_gain.reshape(1, VD), window_order),
        [SMEM] + [VMEM] * 3,
    )
    own = lax.all_to_all(weights, "seq_1", split_axis=0, concat_axis=0, tiled=True).reshape(VD // 2, VD)
    own, normed, member = barrier((own, normed, member))
    other = lax.ppermute(own, "seq_2", [(0, 1), (1, 0)])
    partial = call(
        vision_kernel, sds((FPATCH, VD), bf16), (place, normed, own, other, member), [SMEM] + [VMEM] * 4
    )

    partial, patches, place, merge_gain = barrier((partial, patches, place, merge_gain))
    source, gains, turn = call(
        residual_kernel,
        (sds((UNITS, VD), f32), sds((1, VD), f32), sds((VD // 2, VD // 2), bf16)),
        (place, patches, merge_gain.reshape(1, VD)),
        [SMEM] + [VMEM] * 2,
    )
    partial = lax.all_to_all(
        partial.reshape(NX, UNITS, VD), "head", split_axis=0, concat_axis=0, tiled=True
    ).reshape(FPATCH, VD)
    partial, far, source, gains, turn = barrier((partial, far, source, gains, turn))
    far_other = lax.ppermute(far, "seq_2", [(0, 1), (1, 0)])
    merged = call(merge_kernel, sds((UNITS, VD), bf16), (partial, source, gains, turn))
    merged = lax.all_gather(merged, "head", axis=0, tiled=True)
    visual = call(visual_kernel, sds((LAYER, UNITS, 512), bf16), (merged, far, far_other), vmem=24 << 20)
    asked = far[:, -16:-8].reshape(NZ * 8, 512)
    visual = lax.all_to_all(
        visual, ("seq_1", "seq_2"), split_axis=0, concat_axis=0, tiled=True
    ).reshape(LAYER * UNITS, 512)
    sent = call(
        attend_kernel,
        sds((NZ * SENT, HD), bf16),
        (place, visual, asked, frame_range),
        [SMEM] + [VMEM] * 3,
    )
    sent, queries, suffix_kv, question_lengths = barrier((sent, queries, suffix_kv, question_lengths))
    got = lax.all_to_all(
        sent.reshape(NZ, SENT, HD), "seq_0", split_axis=0, concat_axis=0, tiled=True
    ).reshape(-1, HD)
    mixed, level = call(
        suffix_kernel,
        (sds((4 * GROUP, HD), f32), sds((4 * GROUP, HD), f32)),
        (question_lengths, queries.reshape(4 * GROUP, HD), suffix_kv.reshape(-1, 512)),
        [SMEM] + [VMEM] * 2,
    )
    return call(answer_kernel, sds((2, 2 * GROUP * HD), bf16), (got, mixed, level))


def solution(mesh):
    torus = Mesh(
        mesh.devices.reshape(NZ, NY, NC, NX), ("seq_0", "seq_1", "seq_2", "head")
    )
    in_specs = (
        P(SEQ, None),
        P(),
        P(SEQ, None, "head"),
        P("head", SEQ),
        P(SEQ, None),
        P(),
        P(SEQ, None, "head"),
        P(SEQ, "head"),
        P(SEQ, None, None, "head"),
        P(SEQ),
        P(),
    )
    return jax.shard_map(
        on_device, mesh=torus, in_specs=in_specs, out_specs=P(SEQ, "head"), check_vma=False
    )
```

```python
import jax
import jax.numpy as jnp
from jax import lax
from jax.experimental import pallas as pl
from jax.experimental.pallas import tpu as pltpu
from jax.sharding import Mesh
from jax.sharding import PartitionSpec as P

VD = 1280
VH = 16
HD = 128
FPATCH = 256
WIN = 64
SEQ = ("seq_0", "seq_1", "seq_2")
NZ, NY, NC, NX = 16, 4, 2, 4
ROWS = VD // (NZ * NY * NC)
PACKED = 24
COLS = VD // NX
HEAD = VD // VH
HEADS = COLS // HEAD
UNITS = FPATCH // 4
GROUP = 8
LAYER = NY * NC
NEGATIVE = -1e30
f32 = jnp.float32
bf16 = jnp.bfloat16


def dot(a, b):
    return lax.dot_general(a, b, (((1,), (0,)), ((), ())), preferred_element_type=f32)


def dot_t(a, b):
    return lax.dot_general(a, b, (((1,), (1,)), ((), ())), preferred_element_type=f32)


def iota(shape, dim):
    return lax.broadcasted_iota(jnp.int32, shape, dim)


def one_hot(condition):
    return jnp.where(condition, 1.0, 0.0).astype(bf16)


def call(body, outs, operands, specs=None, vmem=24 << 20):
    vm = pl.BlockSpec(memory_space=pltpu.VMEM)
    return pl.pallas_call(
        body,
        out_shape=outs,
        in_specs=specs or [vm] * len(operands),
        out_specs=jax.tree.map(lambda _: vm, outs),
        compiler_params=pltpu.CompilerParams(vmem_limit_bytes=vmem),
    )(*operands)


VMEM = pl.BlockSpec(memory_space=pltpu.VMEM)
SMEM = pl.BlockSpec(memory_space=pltpu.SMEM)


def near_kernel(weights_ref, out_ref):
    for part in range(2):
        rows = weights_ref[:, part, :]
        for k in range(NY):
            out_ref[k, :, part * 256 : (part + 1) * 256] = rows


def places():
    at = iota((VD, 1), 0)
    return at // (NY * NC * ROWS), at // (NC * ROWS) % NY, at // ROWS % NC, at % ROWS


def prepare_kernel(place_ref, patches_ref, gain_ref, window_ref, normed_ref, member_ref):
    order = one_hot(iota((VD, VD), 1) == gathered(place_ref[2]))
    source = patches_ref[...].astype(f32)
    scale = lax.rsqrt(jnp.mean(source * source, axis=-1, keepdims=True) + 1e-06)
    normed = (source * scale * gain_ref[...]).astype(bf16)
    normed_ref[...] = dot(normed, order).astype(bf16)
    member = one_hot(window_ref[...] == iota((FPATCH, UNITS), 0) // 4)
    shape = (UNITS, 128)
    member_ref[...] = dot(member, one_hot(iota(shape, 0) // (WIN // 4) == iota(shape, 1))).astype(bf16)


def gathered(core):
    z, y, c, r = places()
    return ((c + core) % NC) * (VD // NC) + (y * NZ + z) * ROWS + r


def residual_kernel(place_ref, patches_ref, gain_ref, turn_ref, gains_ref):
    core = place_ref[2]
    order = one_hot(iota((VD, VD), 1) == gathered(core))
    shape = (UNITS, FPATCH)
    pick = one_hot(iota(shape, 1) == iota(shape, 0) * 4 + place_ref[3])
    turn_ref[VD:] = dot(dot(pick, patches_ref[...]).astype(bf16), order).astype(bf16)
    gain = gain_ref[...]
    high = gain.astype(bf16).astype(f32)
    middle = (gain - high).astype(bf16).astype(f32)
    low = gain - high - middle
    part = iota((8, 1), 0)
    parts = jnp.where(part == 0, high, jnp.where(part == 1, middle, jnp.where(part == 2, low, 0.0)))
    gains_ref[...] = jnp.sum(dot(parts.astype(bf16), order), axis=0, keepdims=True)
    row = iota((VD, 1), 0)
    c, y, z, r = row // (VD // NC), row // (NZ * ROWS) % NY, row // ROWS % NZ, row % ROWS
    target = ((y // 2 + core) % NC) * (VD // NC) + ((z * 2 + y % 2) * NC + (c + core) % NC) * ROWS + r
    turn_ref[:VD] = one_hot(iota((VD, VD), 1) == target)


def side_by_side(value):
    return jnp.concatenate([value[:, b * HD : (b + 1) * HD] for b in range(4)], axis=0)


def suffix_kernel(length_ref, asking_ref, suffix_ref, mixed_ref, level_ref):
    asking = side_by_side(asking_ref[...])
    count = asking.shape[0]
    span = suffix_ref.shape[0] // 2
    row = iota((count, 1), 0)
    even = row % 4 < 2
    second = row // 4 % 2
    scores = jnp.where(even, dot_t(asking, suffix_ref[:, 0:128]), dot_t(asking, suffix_ref[:, 128:256]))
    col = iota((1, 2 * span), 1)
    length = jnp.where(second == 0, length_ref[0], length_ref[1])
    live = (col // span == second) & (col % span < length)
    scores = jnp.where(live, scores * HD ** (-0.5), NEGATIVE)
    highest = jnp.max(scores, axis=-1, keepdims=True)
    weights = jnp.exp(scores - highest)
    total = jnp.sum(weights, axis=-1, keepdims=True)
    weights = weights.astype(bf16)
    mixed_ref[...] = jnp.where(even, dot(weights, suffix_ref[:, 256:384]), dot(weights, suffix_ref[:, 384:512]))
    level_ref[...] = jnp.where(iota((1, HD), 1) == 0, highest, total)


def compact_kernel(got_ref, weights_ref):
    got = got_ref[...]
    shape = (NZ * ROWS, NZ * PACKED)
    row, col = iota(shape, 0), iota(shape, 1)
    for half in range(2):
        pick = one_hot(col == (row // ROWS) * PACKED + half * ROWS + row % ROWS)
        weights = dot(pick, got).astype(bf16)
        for k in range(NY):
            weights_ref[k, :, half * 640 : (half + 1) * 640] = weights


def vision_kernel(normed_ref, own_ref, other_ref, member_ref, out_ref):
    wide = 1024
    half = VD // 2
    projected = dot(normed_ref[:, :half], own_ref[:, :wide]) + dot(normed_ref[:, half:], other_ref[:, :wide])
    projected = projected.astype(bf16).astype(f32)
    query = pltpu.roll(projected[:, 0:384], 64, 1)
    key = projected[:, 256:640].astype(bf16)
    value = projected[:, 640:1024]
    together = dot_t(member_ref[...], member_ref[...]) > 0.5
    lane = iota((1, 384), 1)
    mixed = jnp.zeros((FPATCH, 384), f32)
    for h in range(HEADS):
        at = 64 + h * HEAD
        asking = jnp.where((lane >= at) & (lane < at + HEAD), query, 0.0).astype(bf16)
        scores = dot_t(asking, key) * HEAD ** (-0.5)
        scores = jnp.where(together, scores, NEGATIVE)
        weights = jnp.exp(scores - jnp.max(scores, axis=-1, keepdims=True))
        weights = (weights / jnp.sum(weights, axis=-1, keepdims=True)).astype(bf16)
        at = h * HEAD
        mixed += dot(weights, jnp.where((lane >= at) & (lane < at + HEAD), value, 0.0).astype(bf16))
    mixed = pltpu.roll(mixed, 64, 1).astype(bf16)
    shape = (FPATCH, FPATCH)
    row, col = iota(shape, 0), iota(shape, 1)
    mixed = dot(one_hot(col == (row % UNITS) * 4 + row // UNITS), mixed).astype(bf16)
    out_ref[:, :half] = dot_t(mixed, own_ref[:, 896:1280]).astype(bf16)
    out_ref[:, half:] = dot_t(mixed, other_ref[:, 896:1280]).astype(bf16)


def merge_kernel(got_ref, gain_ref, turn_ref, out_ref):
    hidden = turn_ref[VD:].astype(f32)
    for k in range(NX):
        hidden += got_ref[k * UNITS : (k + 1) * UNITS].astype(f32)
    scale = lax.rsqrt(jnp.mean(hidden * hidden, axis=-1, keepdims=True) + 1e-06)
    merged = (hidden * scale * gain_ref[...]).astype(bf16)
    out_ref[...] = dot(merged, turn_ref[:VD]).astype(bf16)


def visual_kernel(merged_ref, own_ref, other_ref, out_ref):
    rows = 4 * NY * ROWS
    half = VD // 2
    total = jnp.zeros((UNITS, 512), f32)
    for i in range(4):
        merged = merged_ref[i * UNITS : (i + 1) * UNITS]
        for part, ref in ((merged[:, :half], own_ref), (merged[:, half:], other_ref)):
            weights = jnp.concatenate([ref[i * 4 + k, :rows] for k in range(4)], axis=0)
            total += dot(part, weights)
    visual = total.astype(bf16)
    for k in range(LAYER):
        out_ref[k] = visual


def attend_kernel(place_ref, visual_ref, asked_ref, range_ref, out_ref):
    layer, inner = place_ref[0], place_ref[1]
    count = NZ * 4 * GROUP
    tokens = LAYER * UNITS
    asking = side_by_side(asked_ref[...])
    row = iota((count, 1), 0)
    even = row % 4 < 2
    question = ((row // 8) % NZ * LAYER + inner) * 2 + (row // 4) % 2
    pick = one_hot(iota((count, 256), 1) == question)
    bounds = dot(pick, range_ref[...].astype(f32).astype(bf16))
    lower, upper = bounds[:, 0:1], bounds[:, 1:2]
    frame = (layer * LAYER + iota((1, tokens), 1) // UNITS).astype(f32)
    live = (frame >= lower) & (frame < upper)
    scores = jnp.where(even, dot_t(asking, visual_ref[:, 0:128]), dot_t(asking, visual_ref[:, 128:256]))
    scores = jnp.where(live, scores * HD ** (-0.5), NEGATIVE)
    highest = jnp.max(scores, axis=-1, keepdims=True)
    weights = jnp.exp(scores - highest)
    total = jnp.sum(weights, axis=-1, keepdims=True)
    weights = weights.astype(bf16)
    mixed = jnp.where(even, dot(weights, visual_ref[:, 256:384]), dot(weights, visual_ref[:, 384:512]))
    mixed = mixed / total
    level = highest + jnp.log(total)
    high = level.astype(bf16).astype(f32)
    middle = (level - high).astype(bf16).astype(f32)
    low = level - high - middle
    lane = iota((1, HD), 1)
    block = row // (NZ * 8)
    levels = jnp.where(
        lane == block, high, jnp.where(lane == block + 4, middle, jnp.where(lane == block + 8, low, 0.0))
    )
    blocks = [slice(b * NZ * 8, (b + 1) * NZ * 8) for b in range(4)]
    for b in range(4):
        out_ref[:, b * HD : (b + 1) * HD] = mixed[blocks[b]].astype(bf16)
    out_ref[:, 4 * HD :] = sum(levels[at] for at in blocks).astype(bf16)


def answer_kernel(got_ref, mixed_ref, level_ref, out_ref):
    got = got_ref[...].astype(f32)
    count = 8
    lane = iota((1, HD), 1)
    answers = []
    for b in range(4):
        at = slice(b * count, (b + 1) * count)
        highest, total = level_ref[at, 0:1], level_ref[at, 1:2]
        mine = (lane < 12) & (lane % 4 == b)
        level = jnp.sum(jnp.where(mine, got[:, 4 * HD :], 0.0), axis=-1, keepdims=True)
        levels = [level[k * count : (k + 1) * count] for k in range(NZ)]
        top = highest
        for k in range(NZ):
            top = jnp.maximum(top, levels[k])
        share = jnp.exp(highest - top)
        mixed = mixed_ref[at] * share
        total = total * share
        for k in range(NZ):
            share = jnp.exp(levels[k] - top)
            mixed += got[k * count : (k + 1) * count, b * HD : (b + 1) * HD] * share
            total += share
        answers.append(mixed / total)
    answers = jnp.concatenate(answers, axis=1)
    for a in range(4):
        pair = jnp.concatenate([answers[a : a + 1], answers[4 + a : 5 + a]], axis=0)
        out_ref[:, a * 512 : (a + 1) * 512] = pair.astype(bf16)


def on_device(
    patches,
    norm_gain,
    w_qkv,
    w_out,
    window_order,
    merge_gain,
    w_kv,
    queries,
    suffix_kv,
    question_lengths,
    frame_range,
):
    sds = jax.ShapeDtypeStruct
    barrier = lax.optimization_barrier
    layer = lax.axis_index("seq_0")
    inner = lax.axis_index(("seq_1", "seq_2"))
    place = jnp.stack([layer, inner, lax.axis_index("seq_2"), lax.axis_index("head")])

    near = call(near_kernel, sds((NY, 4 * ROWS, 512), bf16), (w_kv,))
    near = lax.all_to_all(near, "seq_1", split_axis=0, concat_axis=0, tiled=True).reshape(-1, 512)
    packed = jnp.concatenate([w_qkv.reshape(ROWS, 3 * COLS), w_out.T], axis=1)
    packed = jnp.concatenate(
        [packed[:, :640], packed[:, 640:], jnp.zeros((PACKED - 2 * ROWS, 640), bf16)], axis=0
    )
    packed, near = barrier((packed, near))
    near = jnp.concatenate([near, queries.reshape(8, 512), jnp.zeros((8, 512), bf16)], axis=0)
    far = lax.all_gather(near, "seq_0", axis=0)
    got = lax.all_gather(packed, "seq_0", axis=0, tiled=True)
    weights = call(compact_kernel, sds((NY, NZ * ROWS, VD), bf16), (got,))

    weights, patches, place, norm_gain, window_order = barrier((weights, patches, place, norm_gain, window_order))
    normed, member = call(
        prepare_kernel,
        (sds((FPATCH, VD), bf16), sds((FPATCH, 128), bf16)),
        (place, patches, norm_gain.reshape(1, VD), window_order),
        [SMEM] + [VMEM] * 3,
    )
    own = lax.all_to_all(weights, "seq_1", split_axis=0, concat_axis=0, tiled=True).reshape(VD // 2, VD)
    own, normed, member = barrier((own, normed, member))
    other = lax.ppermute(own, "seq_2", [(0, 1), (1, 0)])
    partial = call(
        vision_kernel, sds((FPATCH, VD), bf16), (normed, own, other, member)
    )

    partial, patches, place, merge_gain = barrier((partial, patches, place, merge_gain))
    turn, gains = call(
        residual_kernel,
        (sds((VD + UNITS, VD), bf16), sds((1, VD), f32)),
        (place, patches, merge_gain.reshape(1, VD)),
        [SMEM] + [VMEM] * 2,
    )
    partial = lax.all_to_all(
        partial.reshape(NX, UNITS, VD), "head", split_axis=0, concat_axis=0, tiled=True
    ).reshape(FPATCH, VD)
    partial, far, gains, turn = barrier((partial, far, gains, turn))
    far_other = lax.ppermute(far, "seq_2", [(0, 1), (1, 0)])
    merged = call(merge_kernel, sds((UNITS, VD), bf16), (partial, gains, turn))
    merged = lax.all_gather(merged, "head", axis=0, tiled=True)
    visual = call(visual_kernel, sds((LAYER, UNITS, 512), bf16), (merged, far, far_other), vmem=24 << 20)
    asked = far[:, -16:-8].reshape(NZ * 8, 512)
    visual = lax.all_to_all(
        visual, ("seq_1", "seq_2"), split_axis=0, concat_axis=0, tiled=True
    ).reshape(LAYER * UNITS, 512)
    sent = call(
        attend_kernel,
        sds((NZ * 8, 5 * HD), bf16),
        (place, visual, asked, frame_range),
        [SMEM] + [VMEM] * 3,
    )
    sent, queries, suffix_kv, question_lengths = barrier((sent, queries, suffix_kv, question_lengths))
    got = lax.all_to_all(
        sent.reshape(NZ, 8, 5 * HD), "seq_0", split_axis=0, concat_axis=0, tiled=True
    ).reshape(-1, 5 * HD)
    mixed, level = call(
        suffix_kernel,
        (sds((4 * GROUP, HD), f32), sds((4 * GROUP, HD), f32)),
        (question_lengths, queries.reshape(8, 512), suffix_kv.reshape(-1, 512)),
        [SMEM] + [VMEM] * 2,
    )
    return call(answer_kernel, sds((2, 2 * GROUP * HD), bf16), (got, mixed, level))


def solution(mesh):
    torus = Mesh(
        mesh.devices.reshape(NZ, NY, NC, NX), ("seq_0", "seq_1", "seq_2", "head")
    )
    in_specs = (
        P(SEQ, None),
        P(),
        P(SEQ, None, "head"),
        P("head", SEQ),
        P(SEQ, None),
        P(),
        P(SEQ, None, "head"),
        P(SEQ, "head"),
        P(SEQ, None, None, "head"),
        P(SEQ),
        P(),
    )
    return jax.shard_map(
        on_device, mesh=torus, in_specs=in_specs, out_specs=P(SEQ, "head"), check_vma=False
    )
```

```python
import jax
import jax.numpy as jnp
from jax import lax
from jax.experimental import pallas as pl
from jax.experimental.pallas import tpu as pltpu
from jax.sharding import Mesh
from jax.sharding import PartitionSpec as P

VD = 1280
VH = 16
HD = 128
FPATCH = 256
WIN = 64
SEQ = ("seq_0", "seq_1", "seq_2")
NZ, NY, NC, NX = 16, 4, 2, 4
ROWS = VD // (NZ * NY * NC)
PACKED = 24
COLS = VD // NX
HEAD = VD // VH
HEADS = COLS // HEAD
UNITS = FPATCH // 4
GROUP = 8
LAYER = NY * NC
NEGATIVE = -1e30
f32 = jnp.float32
bf16 = jnp.bfloat16


def dot(a, b):
    return lax.dot_general(a, b, (((1,), (0,)), ((), ())), preferred_element_type=f32)


def dot_t(a, b):
    return lax.dot_general(a, b, (((1,), (1,)), ((), ())), preferred_element_type=f32)


def iota(shape, dim):
    return lax.broadcasted_iota(jnp.int32, shape, dim)


def one_hot(condition):
    return jnp.where(condition, 1.0, 0.0).astype(bf16)


def call(body, outs, operands, specs=None, vmem=24 << 20):
    vm = pl.BlockSpec(memory_space=pltpu.VMEM)
    return pl.pallas_call(
        body,
        out_shape=outs,
        in_specs=specs or [vm] * len(operands),
        out_specs=jax.tree.map(lambda _: vm, outs),
        compiler_params=pltpu.CompilerParams(vmem_limit_bytes=vmem),
    )(*operands)


VMEM = pl.BlockSpec(memory_space=pltpu.VMEM)
SMEM = pl.BlockSpec(memory_space=pltpu.SMEM)


def places():
    at = iota((VD, 1), 0)
    return at // (NY * NC * ROWS), at // (NC * ROWS) % NY, at // ROWS % NC, at % ROWS


def prepare_kernel(place_ref, patches_ref, gain_ref, window_ref, normed_ref, member_ref):
    order = one_hot(iota((VD, VD), 1) == gathered(place_ref[2]))
    source = patches_ref[...].astype(f32)
    scale = lax.rsqrt(jnp.mean(source * source, axis=-1, keepdims=True) + 1e-06)
    normed = (source * scale * gain_ref[...]).astype(bf16)
    normed_ref[...] = dot(normed, order).astype(bf16)
    member = one_hot(window_ref[...] == iota((FPATCH, UNITS), 0) // 4)
    shape = (UNITS, 128)
    member_ref[...] = dot(member, one_hot(iota(shape, 0) // (WIN // 4) == iota(shape, 1))).astype(bf16)


def gathered(core):
    z, y, c, r = places()
    return ((c + core) % NC) * (VD // NC) + (y * NZ + z) * ROWS + r


def residual_kernel(place_ref, patches_ref, gain_ref, turn_ref, gains_ref):
    core = place_ref[2]
    half = VD // 2
    z, y, c, r = places()
    target = (y // 2) * half + (((c + core) % NC * 2 + y % 2) * NZ + z) * ROWS + r
    order = one_hot(iota((VD, VD), 1) == target)
    shape = (UNITS, FPATCH)
    pick = one_hot(iota(shape, 1) == iota(shape, 0) * 4 + place_ref[3])
    source = dot(dot(pick, patches_ref[...]).astype(bf16), order).astype(bf16)
    turn_ref[half : half + UNITS] = source[:, :half]
    turn_ref[half + UNITS :] = source[:, half:]
    gain = gain_ref[...]
    high = gain.astype(bf16).astype(f32)
    middle = (gain - high).astype(bf16).astype(f32)
    low = gain - high - middle
    part = iota((8, 1), 0)
    parts = jnp.where(part == 0, high, jnp.where(part == 1, middle, jnp.where(part == 2, low, 0.0)))
    gains_ref[...] = jnp.sum(dot(parts.astype(bf16), order), axis=0, keepdims=True)
    row = iota((half, 1), 0)
    c, y, z, r = row // (2 * NZ * ROWS), row // (NZ * ROWS) % 2, row // ROWS % NZ, row % ROWS
    target = ((z * 2 + y) * NC + (c + core) % NC) * ROWS + r
    turn_ref[:half] = one_hot(iota((half, half), 1) == target)


def side_by_side(value):
    return jnp.concatenate([value[:, b * HD : (b + 1) * HD] for b in range(4)], axis=0)


def suffix_kernel(length_ref, asking_ref, suffix_ref, mixed_ref, level_ref):
    asking = side_by_side(asking_ref[...])
    count = asking.shape[0]
    span = suffix_ref.shape[0] // 2
    row = iota((count, 1), 0)
    even = row % 4 < 2
    second = row // 4 % 2
    scores = jnp.where(even, dot_t(asking, suffix_ref[:, 0:128]), dot_t(asking, suffix_ref[:, 128:256]))
    col = iota((1, 2 * span), 1)
    length = jnp.where(second == 0, length_ref[0], length_ref[1])
    live = (col // span == second) & (col % span < length)
    scores = jnp.where(live, scores * HD ** (-0.5), NEGATIVE)
    highest = jnp.max(scores, axis=-1, keepdims=True)
    weights = jnp.exp(scores - highest)
    total = jnp.sum(weights, axis=-1, keepdims=True)
    weights = weights.astype(bf16)
    mixed_ref[...] = jnp.where(even, dot(weights, suffix_ref[:, 256:384]), dot(weights, suffix_ref[:, 384:512]))
    level_ref[...] = jnp.where(iota((1, HD), 1) == 0, highest, total)


def compact_kernel(got_ref, weights_ref):
    got = got_ref[...]
    shape = (NZ * ROWS, NZ * PACKED)
    row, col = iota(shape, 0), iota(shape, 1)
    for half in range(2):
        pick = one_hot(col == (row // ROWS) * PACKED + half * ROWS + row % ROWS)
        weights = dot(pick, got).astype(bf16)
        for k in range(NY):
            weights_ref[k, :, half * 640 : (half + 1) * 640] = weights


def vision_kernel(normed_ref, own_ref, other_ref, member_ref, out_ref):
    half = VD // 2
    projected = dot(normed_ref[:, :half], own_ref[:, :1024]) + dot(normed_ref[:, half:], other_ref[:, :1024])
    projected = projected.astype(bf16).astype(f32)
    query = pltpu.roll(projected[:, 0:384], 64, 1)
    key = projected[:, 256:640].astype(bf16)
    value = projected[:, 640:1024]
    together = dot_t(member_ref[...], member_ref[...]) > 0.5
    lane = iota((1, 384), 1)
    mixed = jnp.zeros((FPATCH, 384), f32)
    for h in range(HEADS):
        at = 64 + h * HEAD
        asking = jnp.where((lane >= at) & (lane < at + HEAD), query, 0.0).astype(bf16)
        scores = dot_t(asking, key) * HEAD ** (-0.5)
        scores = jnp.where(together, scores, NEGATIVE)
        weights = jnp.exp(scores - jnp.max(scores, axis=-1, keepdims=True))
        weights = (weights / jnp.sum(weights, axis=-1, keepdims=True)).astype(bf16)
        at = h * HEAD
        mixed += dot(weights, jnp.where((lane >= at) & (lane < at + HEAD), value, 0.0).astype(bf16))
    mixed = pltpu.roll(mixed, 64, 1).astype(bf16)
    shape = (FPATCH, FPATCH)
    row, col = iota(shape, 0), iota(shape, 1)
    mixed = dot(one_hot(col == (row % UNITS) * 4 + row // UNITS), mixed).astype(bf16)
    for part in range(2):
        rows = slice(part * half // 2, (part + 1) * half // 2)
        weights = jnp.concatenate([own_ref[rows, 896:1280], other_ref[rows, 896:1280]], axis=0)
        out_ref[:, part * half : (part + 1) * half] = dot_t(mixed, weights).astype(bf16)


def merge_kernel(place_ref, got_ref, gain_ref, turn_ref, out_ref):
    half = VD // 2
    hidden = jnp.concatenate([turn_ref[half : half + UNITS], turn_ref[half + UNITS :]], axis=1).astype(f32)
    for k in range(NX):
        hidden += got_ref[k * UNITS : (k + 1) * UNITS].astype(f32)
    scale = lax.rsqrt(jnp.mean(hidden * hidden, axis=-1, keepdims=True) + 1e-06)
    merged = (hidden * scale * gain_ref[...]).astype(bf16)
    left = dot(merged[:, :half], turn_ref[:half])
    right = dot(merged[:, half:], turn_ref[:half])
    first = place_ref[2] == 0
    out_ref[:, :half] = jnp.where(first, left, right).astype(bf16)
    out_ref[:, half:] = jnp.where(first, right, left).astype(bf16)


def visual_kernel(merged_ref, own_ref, other_ref, out_ref):
    rows = 4 * NY * ROWS
    half = VD // 2
    total = jnp.zeros((UNITS, 512), f32)
    for i in range(4):
        merged = merged_ref[i * UNITS : (i + 1) * UNITS]
        for part, ref in ((merged[:, :half], own_ref), (merged[:, half:], other_ref)):
            weights = jnp.concatenate([ref[i * 4 + k, :rows] for k in range(4)], axis=0)
            total += dot(part, weights)
    visual = total.astype(bf16)
    for k in range(LAYER):
        out_ref[k] = visual


def attend_kernel(place_ref, visual_ref, asked_ref, range_ref, out_ref):
    layer, inner = place_ref[0], place_ref[1]
    count = NZ * 4 * GROUP
    tokens = LAYER * UNITS
    asking = side_by_side(asked_ref[...])
    row = iota((count, 1), 0)
    even = row % 4 < 2
    question = ((row // 8) % NZ * LAYER + inner) * 2 + (row // 4) % 2
    pick = one_hot(iota((count, 256), 1) == question)
    bounds = dot(pick, range_ref[...].astype(f32).astype(bf16))
    lower, upper = bounds[:, 0:1], bounds[:, 1:2]
    frame = (layer * LAYER + iota((1, tokens), 1) // UNITS).astype(f32)
    live = (frame >= lower) & (frame < upper)
    scores = jnp.where(even, dot_t(asking, visual_ref[:, 0:128]), dot_t(asking, visual_ref[:, 128:256]))
    scores = jnp.where(live, scores * HD ** (-0.5), NEGATIVE)
    highest = jnp.max(scores, axis=-1, keepdims=True)
    weights = jnp.exp(scores - highest)
    total = jnp.sum(weights, axis=-1, keepdims=True)
    weights = weights.astype(bf16)
    mixed = jnp.where(even, dot(weights, visual_ref[:, 256:384]), dot(weights, visual_ref[:, 384:512]))
    mixed = mixed / total
    level = highest + jnp.log(total)
    high = level.astype(bf16).astype(f32)
    middle = (level - high).astype(bf16).astype(f32)
    low = level - high - middle
    lane = iota((1, HD), 1)
    block = row // (NZ * 8)
    levels = jnp.where(
        lane == block, high, jnp.where(lane == block + 4, middle, jnp.where(lane == block + 8, low, 0.0))
    )
    blocks = [slice(b * NZ * 8, (b + 1) * NZ * 8) for b in range(4)]
    for b in range(4):
        out_ref[:, b * HD : (b + 1) * HD] = mixed[blocks[b]].astype(bf16)
    out_ref[:, 4 * HD :] = sum(levels[at] for at in blocks).astype(bf16)


def answer_kernel(got_ref, mixed_ref, level_ref, out_ref):
    got = got_ref[...].astype(f32)
    count = 8
    lane = iota((1, HD), 1)
    answers = []
    for b in range(4):
        at = slice(b * count, (b + 1) * count)
        highest, total = level_ref[at, 0:1], level_ref[at, 1:2]
        mine = (lane < 12) & (lane % 4 == b)
        level = jnp.sum(jnp.where(mine, got[:, 4 * HD :], 0.0), axis=-1, keepdims=True)
        levels = [level[k * count : (k + 1) * count] for k in range(NZ)]
        top = highest
        for k in range(NZ):
            top = jnp.maximum(top, levels[k])
        share = jnp.exp(highest - top)
        mixed = mixed_ref[at] * share
        total = total * share
        for k in range(NZ):
            share = jnp.exp(levels[k] - top)
            mixed += got[k * count : (k + 1) * count, b * HD : (b + 1) * HD] * share
            total += share
        answers.append(mixed / total)
    answers = jnp.concatenate(answers, axis=1)
    for a in range(4):
        pair = jnp.concatenate([answers[a : a + 1], answers[4 + a : 5 + a]], axis=0)
        out_ref[:, a * 512 : (a + 1) * 512] = pair.astype(bf16)


def on_device(
    patches,
    norm_gain,
    w_qkv,
    w_out,
    window_order,
    merge_gain,
    w_kv,
    queries,
    suffix_kv,
    question_lengths,
    frame_range,
):
    sds = jax.ShapeDtypeStruct
    barrier = lax.optimization_barrier
    layer = lax.axis_index("seq_0")
    inner = lax.axis_index(("seq_1", "seq_2"))
    place = jnp.stack([layer, inner, lax.axis_index("seq_2"), lax.axis_index("head")])

    near = jnp.broadcast_to(w_kv[None], (NY, *w_kv.shape))
    near = lax.all_to_all(near, "seq_1", split_axis=0, concat_axis=0, tiled=True).reshape(-1, 512)
    packed = jnp.concatenate([w_qkv.reshape(ROWS, 3 * COLS), w_out.T], axis=1)
    packed = jnp.concatenate(
        [packed[:, :640], packed[:, 640:], jnp.zeros((PACKED - 2 * ROWS, 640), bf16)], axis=0
    )
    packed, near = barrier((packed, near))
    near = jnp.concatenate([near, queries.reshape(8, 512), jnp.zeros((8, 512), bf16)], axis=0)
    far = lax.all_gather(near, "seq_0", axis=0)
    got = lax.all_gather(packed, "seq_0", axis=0, tiled=True)
    weights = call(compact_kernel, sds((NY, NZ * ROWS, VD), bf16), (got,))

    weights, patches, place, norm_gain, window_order = barrier((weights, patches, place, norm_gain, window_order))
    normed, member = call(
        prepare_kernel,
        (sds((FPATCH, VD), bf16), sds((FPATCH, 128), bf16)),
        (place, patches, norm_gain.reshape(1, VD), window_order),
        [SMEM] + [VMEM] * 3,
    )
    own = lax.all_to_all(weights, "seq_1", split_axis=0, concat_axis=0, tiled=True).reshape(VD // 2, VD)
    own, normed, member = barrier((own, normed, member))
    other = lax.ppermute(own, "seq_2", [(0, 1), (1, 0)])
    partial = call(
        vision_kernel, sds((FPATCH, VD), bf16), (normed, own, other, member)
    )

    partial, patches, place, merge_gain = barrier((partial, patches, place, merge_gain))
    turn, gains = call(
        residual_kernel,
        (sds((VD // 2 + 2 * UNITS, VD // 2), bf16), sds((1, VD), f32)),
        (place, patches, merge_gain.reshape(1, VD)),
        [SMEM] + [VMEM] * 2,
    )
    partial = lax.all_to_all(
        partial.reshape(NX, UNITS, VD), "head", split_axis=0, concat_axis=0, tiled=True
    ).reshape(FPATCH, VD)
    partial, far, gains, turn = barrier((partial, far, gains, turn))
    far_other = lax.ppermute(far, "seq_2", [(0, 1), (1, 0)])
    merged = call(merge_kernel, sds((UNITS, VD), bf16), (place, partial, gains, turn), [SMEM] + [VMEM] * 3)
    merged = lax.all_gather(merged, "head", axis=0, tiled=True)
    visual = call(visual_kernel, sds((LAYER, UNITS, 512), bf16), (merged, far, far_other), vmem=24 << 20)
    asked = far[:, -16:-8].reshape(NZ * 8, 512)
    visual = lax.all_to_all(
        visual, ("seq_1", "seq_2"), split_axis=0, concat_axis=0, tiled=True
    ).reshape(LAYER * UNITS, 512)
    sent = call(
        attend_kernel,
        sds((NZ * 8, 5 * HD), bf16),
        (place, visual, asked, frame_range),
        [SMEM] + [VMEM] * 3,
    )
    sent, queries, suffix_kv, question_lengths = barrier((sent, queries, suffix_kv, question_lengths))
    got = lax.all_to_all(
        sent.reshape(NZ, 8, 5 * HD), "seq_0", split_axis=0, concat_axis=0, tiled=True
    ).reshape(-1, 5 * HD)
    mixed, level = call(
        suffix_kernel,
        (sds((4 * GROUP, HD), f32), sds((4 * GROUP, HD), f32)),
        (question_lengths, queries.reshape(8, 512), suffix_kv.reshape(-1, 512)),
        [SMEM] + [VMEM] * 2,
    )
    return call(answer_kernel, sds((2, 2 * GROUP * HD), bf16), (got, mixed, level))


def solution(mesh):
    torus = Mesh(
        mesh.devices.reshape(NZ, NY, NC, NX), ("seq_0", "seq_1", "seq_2", "head")
    )
    in_specs = (
        P(SEQ, None),
        P(),
        P(SEQ, None, "head"),
        P("head", SEQ),
        P(SEQ, None),
        P(),
        P(SEQ, None, "head"),
        P(SEQ, "head"),
        P(SEQ, None, None, "head"),
        P(SEQ),
        P(),
    )
    return jax.shard_map(
        on_device, mesh=torus, in_specs=in_specs, out_specs=P(SEQ, "head"), check_vma=False
    )
```

```python
import jax
import jax.numpy as jnp
from jax import lax
from jax.experimental import pallas as pl
from jax.experimental.pallas import tpu as pltpu
from jax.sharding import Mesh
from jax.sharding import PartitionSpec as P

VD = 1280
VH = 16
HD = 128
FPATCH = 256
WIN = 64
SEQ = ("seq_0", "seq_1", "seq_2")
NZ, NY, NC, NX = 16, 4, 2, 4
ROWS = VD // (NZ * NY * NC)
PACKED = 24
COLS = VD // NX
HEAD = VD // VH
HEADS = COLS // HEAD
UNITS = FPATCH // 4
GROUP = 8
LAYER = NY * NC
NEGATIVE = -1e30
TURNS = (("seq_0", "seq_2"), [[z * NC + (z + group) % NC for z in range(NZ)] for group in range(NC)])
f32 = jnp.float32
bf16 = jnp.bfloat16


def dot(a, b):
    return lax.dot_general(a, b, (((1,), (0,)), ((), ())), preferred_element_type=f32)


def dot_t(a, b):
    return lax.dot_general(a, b, (((1,), (1,)), ((), ())), preferred_element_type=f32)


def iota(shape, dim):
    return lax.broadcasted_iota(jnp.int32, shape, dim)


def one_hot(condition):
    return jnp.where(condition, 1.0, 0.0).astype(bf16)


def call(body, outs, operands, specs=None, vmem=24 << 20):
    vm = pl.BlockSpec(memory_space=pltpu.VMEM)
    return pl.pallas_call(
        body,
        out_shape=outs,
        in_specs=specs or [vm] * len(operands),
        out_specs=jax.tree.map(lambda _: vm, outs),
        compiler_params=pltpu.CompilerParams(vmem_limit_bytes=vmem),
    )(*operands)


VMEM = pl.BlockSpec(memory_space=pltpu.VMEM)
SMEM = pl.BlockSpec(memory_space=pltpu.SMEM)


def places():
    at = iota((VD, 1), 0)
    return at // (NY * NC * ROWS), at // (NC * ROWS) % NY, at // ROWS % NC, at % ROWS


def prepare_kernel(place_ref, patches_ref, gain_ref, window_ref, normed_ref, member_ref):
    order = one_hot(iota((VD, VD), 1) == gathered(place_ref[2] + place_ref[0]))
    source = patches_ref[...].astype(f32)
    scale = lax.rsqrt(jnp.mean(source * source, axis=-1, keepdims=True) + 1e-06)
    normed = (source * scale * gain_ref[...]).astype(bf16)
    normed_ref[...] = dot(normed, order).astype(bf16)
    member = one_hot(window_ref[...] == iota((FPATCH, UNITS), 0) // 4)
    shape = (UNITS, 128)
    member_ref[...] = dot(member, one_hot(iota(shape, 0) // (WIN // 4) == iota(shape, 1))).astype(bf16)


def gathered(group):
    z, y, c, r = places()
    return ((c + z + group) % NC) * (VD // NC) + (y * NZ + z) * ROWS + r


def residual_kernel(place_ref, patches_ref, gain_ref, turn_ref, gains_ref):
    group = place_ref[2] + place_ref[0]
    half = VD // 2
    z, y, c, r = places()
    target = (y // 2) * half + (((c + z + group) % NC * 2 + y % 2) * NZ + z) * ROWS + r
    order = one_hot(iota((VD, VD), 1) == target)
    shape = (UNITS, FPATCH)
    pick = one_hot(iota(shape, 1) == iota(shape, 0) * 4 + place_ref[3])
    source = dot(dot(pick, patches_ref[...]).astype(bf16), order).astype(bf16)
    turn_ref[half : half + UNITS] = source[:, :half]
    turn_ref[half + UNITS :] = source[:, half:]
    gain = gain_ref[...]
    high = gain.astype(bf16).astype(f32)
    middle = (gain - high).astype(bf16).astype(f32)
    low = gain - high - middle
    part = iota((8, 1), 0)
    parts = jnp.where(part == 0, high, jnp.where(part == 1, middle, jnp.where(part == 2, low, 0.0)))
    gains_ref[...] = jnp.sum(dot(parts.astype(bf16), order), axis=0, keepdims=True)
    row = iota((half, 1), 0)
    c, y, z, r = row // (2 * NZ * ROWS), row // (NZ * ROWS) % 2, row // ROWS % NZ, row % ROWS
    target = ((z * 2 + y) * NC + (c + z + group) % NC) * ROWS + r
    turn_ref[:half] = one_hot(iota((half, half), 1) == target)


def side_by_side(value):
    return jnp.concatenate([value[:, b * HD : (b + 1) * HD] for b in range(4)], axis=0)


def suffix_kernel(length_ref, asking_ref, suffix_ref, mixed_ref, level_ref):
    asking = side_by_side(asking_ref[...])
    count = asking.shape[0]
    span = suffix_ref.shape[0] // 2
    row = iota((count, 1), 0)
    even = row % 4 < 2
    second = row // 4 % 2
    scores = jnp.where(even, dot_t(asking, suffix_ref[:, 0:128]), dot_t(asking, suffix_ref[:, 128:256]))
    col = iota((1, 2 * span), 1)
    length = jnp.where(second == 0, length_ref[0], length_ref[1])
    live = (col // span == second) & (col % span < length)
    scores = jnp.where(live, scores * HD ** (-0.5), NEGATIVE)
    highest = jnp.max(scores, axis=-1, keepdims=True)
    weights = jnp.exp(scores - highest)
    total = jnp.sum(weights, axis=-1, keepdims=True)
    weights = weights.astype(bf16)
    mixed_ref[...] = jnp.where(even, dot(weights, suffix_ref[:, 256:384]), dot(weights, suffix_ref[:, 384:512]))
    level_ref[...] = jnp.where(iota((1, HD), 1) == 0, highest, total)


def compact_kernel(got_ref, weights_ref):
    got = got_ref[...]
    shape = (NZ * ROWS, NZ * PACKED)
    row, col = iota(shape, 0), iota(shape, 1)
    for half in range(2):
        pick = one_hot(col == (row // ROWS) * PACKED + half * ROWS + row % ROWS)
        weights = dot(pick, got).astype(bf16)
        for k in range(NY):
            weights_ref[k, :, half * 640 : (half + 1) * 640] = weights


def vision_kernel(normed_ref, own_ref, other_ref, member_ref, out_ref):
    half = VD // 2
    projected = dot(normed_ref[:, :half], own_ref[:, :1024]) + dot(normed_ref[:, half:], other_ref[:, :1024])
    projected = projected.astype(bf16).astype(f32)
    query = pltpu.roll(projected[:, 0:384], 64, 1)
    key = projected[:, 256:640].astype(bf16)
    value = projected[:, 640:1024]
    together = dot_t(member_ref[...], member_ref[...]) > 0.5
    lane = iota((1, 384), 1)
    mixed = jnp.zeros((FPATCH, 384), f32)
    for h in range(HEADS):
        at = 64 + h * HEAD
        asking = jnp.where((lane >= at) & (lane < at + HEAD), query, 0.0).astype(bf16)
        scores = dot_t(asking, key) * HEAD ** (-0.5)
        scores = jnp.where(together, scores, NEGATIVE)
        weights = jnp.exp(scores - jnp.max(scores, axis=-1, keepdims=True))
        weights = (weights / jnp.sum(weights, axis=-1, keepdims=True)).astype(bf16)
        at = h * HEAD
        mixed += dot(weights, jnp.where((lane >= at) & (lane < at + HEAD), value, 0.0).astype(bf16))
    mixed = pltpu.roll(mixed, 64, 1).astype(bf16)
    shape = (FPATCH, FPATCH)
    row, col = iota(shape, 0), iota(shape, 1)
    mixed = dot(one_hot(col == (row % UNITS) * 4 + row // UNITS), mixed).astype(bf16)
    for part in range(2):
        rows = slice(part * half // 2, (part + 1) * half // 2)
        weights = jnp.concatenate([own_ref[rows, 896:1280], other_ref[rows, 896:1280]], axis=0)
        out_ref[:, part * half : (part + 1) * half] = dot_t(mixed, weights).astype(bf16)


def merge_kernel(place_ref, got_ref, gain_ref, turn_ref, out_ref):
    half = VD // 2
    hidden = jnp.concatenate([turn_ref[half : half + UNITS], turn_ref[half + UNITS :]], axis=1).astype(f32)
    for k in range(NX):
        hidden += got_ref[k * UNITS : (k + 1) * UNITS].astype(f32)
    scale = lax.rsqrt(jnp.mean(hidden * hidden, axis=-1, keepdims=True) + 1e-06)
    merged = (hidden * scale * gain_ref[...]).astype(bf16)
    left = dot(merged[:, :half], turn_ref[:half])
    right = dot(merged[:, half:], turn_ref[:half])
    first = (iota((1, half), 1) // (4 * NY * ROWS) + place_ref[2] + place_ref[0]) % NC == 0
    out_ref[:, :half] = jnp.where(first, left, right).astype(bf16)
    out_ref[:, half:] = jnp.where(first, right, left).astype(bf16)


def visual_kernel(merged_ref, own_ref, other_ref, out_ref):
    rows = 4 * NY * ROWS
    half = VD // 2
    total = jnp.zeros((UNITS, 512), f32)
    for i in range(4):
        merged = merged_ref[i * UNITS : (i + 1) * UNITS]
        for part, ref in ((merged[:, :half], own_ref), (merged[:, half:], other_ref)):
            weights = jnp.concatenate([ref[i * 4 + k, :rows] for k in range(4)], axis=0)
            total += dot(part, weights)
    visual = total.astype(bf16)
    for k in range(LAYER):
        out_ref[k] = visual


def attend_kernel(place_ref, visual_ref, asked_ref, range_ref, out_ref):
    layer, inner = place_ref[0], place_ref[1]
    group = place_ref[2] + layer
    count = NZ * 4 * GROUP
    tokens = LAYER * UNITS
    asking = side_by_side(asked_ref[...])
    row = iota((count, 1), 0)
    even = row % 4 < 2
    z = row // 8 % NZ
    question = (z * LAYER + inner // NC * NC + (z + group) % NC) * 2 + row // 4 % 2
    pick = one_hot(iota((count, 256), 1) == question)
    bounds = dot(pick, range_ref[...].astype(f32).astype(bf16))
    lower, upper = bounds[:, 0:1], bounds[:, 1:2]
    frame = (layer * LAYER + iota((1, tokens), 1) // UNITS).astype(f32)
    live = (frame >= lower) & (frame < upper)
    scores = jnp.where(even, dot_t(asking, visual_ref[:, 0:128]), dot_t(asking, visual_ref[:, 128:256]))
    scores = jnp.where(live, scores * HD ** (-0.5), NEGATIVE)
    highest = jnp.max(scores, axis=-1, keepdims=True)
    weights = jnp.exp(scores - highest)
    total = jnp.sum(weights, axis=-1, keepdims=True)
    weights = weights.astype(bf16)
    mixed = jnp.where(even, dot(weights, visual_ref[:, 256:384]), dot(weights, visual_ref[:, 384:512]))
    mixed = mixed / total
    level = highest + jnp.log(total)
    high = level.astype(bf16).astype(f32)
    middle = (level - high).astype(bf16).astype(f32)
    low = level - high - middle
    lane = iota((1, HD), 1)
    block = row // (NZ * 8)
    levels = jnp.where(
        lane == block, high, jnp.where(lane == block + 4, middle, jnp.where(lane == block + 8, low, 0.0))
    )
    blocks = [slice(b * NZ * 8, (b + 1) * NZ * 8) for b in range(4)]
    for b in range(4):
        out_ref[:, b * HD : (b + 1) * HD] = mixed[blocks[b]].astype(bf16)
    out_ref[:, 4 * HD :] = sum(levels[at] for at in blocks).astype(bf16)


def answer_kernel(got_ref, mixed_ref, level_ref, out_ref):
    got = got_ref[...].astype(f32)
    count = 8
    lane = iota((1, HD), 1)
    answers = []
    for b in range(4):
        at = slice(b * count, (b + 1) * count)
        highest, total = level_ref[at, 0:1], level_ref[at, 1:2]
        mine = (lane < 12) & (lane % 4 == b)
        level = jnp.sum(jnp.where(mine, got[:, 4 * HD :], 0.0), axis=-1, keepdims=True)
        levels = [level[k * count : (k + 1) * count] for k in range(NZ)]
        top = highest
        for k in range(NZ):
            top = jnp.maximum(top, levels[k])
        share = jnp.exp(highest - top)
        mixed = mixed_ref[at] * share
        total = total * share
        for k in range(NZ):
            share = jnp.exp(levels[k] - top)
            mixed += got[k * count : (k + 1) * count, b * HD : (b + 1) * HD] * share
            total += share
        answers.append(mixed / total)
    answers = jnp.concatenate(answers, axis=1)
    for a in range(4):
        pair = jnp.concatenate([answers[a : a + 1], answers[4 + a : 5 + a]], axis=0)
        out_ref[:, a * 512 : (a + 1) * 512] = pair.astype(bf16)


def on_device(
    patches,
    norm_gain,
    w_qkv,
    w_out,
    window_order,
    merge_gain,
    w_kv,
    queries,
    suffix_kv,
    question_lengths,
    frame_range,
):
    sds = jax.ShapeDtypeStruct
    barrier = lax.optimization_barrier
    layer = lax.axis_index("seq_0")
    inner = lax.axis_index(("seq_1", "seq_2"))
    place = jnp.stack([layer, inner, lax.axis_index("seq_2"), lax.axis_index("head")])

    near = jnp.broadcast_to(w_kv[None], (NY, *w_kv.shape))
    near = lax.all_to_all(near, "seq_1", split_axis=0, concat_axis=0, tiled=True).reshape(-1, 512)
    packed = jnp.concatenate([w_qkv.reshape(ROWS, 3 * COLS), w_out.T], axis=1)
    packed = jnp.concatenate(
        [packed[:, :640], packed[:, 640:], jnp.zeros((PACKED - 2 * ROWS, 640), bf16)], axis=0
    )
    packed, near = barrier((packed, near))
    near = jnp.concatenate([near, queries.reshape(8, 512), jnp.zeros((8, 512), bf16)], axis=0)
    far = lax.all_gather(near, TURNS[0], axis=0, axis_index_groups=TURNS[1])
    got = lax.all_gather(packed, TURNS[0], axis=0, axis_index_groups=TURNS[1], tiled=True)
    weights = call(compact_kernel, sds((NY, NZ * ROWS, VD), bf16), (got,))

    weights, patches, place, norm_gain, window_order = barrier((weights, patches, place, norm_gain, window_order))
    normed, member = call(
        prepare_kernel,
        (sds((FPATCH, VD), bf16), sds((FPATCH, 128), bf16)),
        (place, patches, norm_gain.reshape(1, VD), window_order),
        [SMEM] + [VMEM] * 3,
    )
    own = lax.all_to_all(weights, "seq_1", split_axis=0, concat_axis=0, tiled=True).reshape(VD // 2, VD)
    own, normed, member = barrier((own, normed, member))
    other = lax.ppermute(own, "seq_2", [(0, 1), (1, 0)])
    partial = call(
        vision_kernel, sds((FPATCH, VD), bf16), (normed, own, other, member)
    )

    partial, patches, place, merge_gain = barrier((partial, patches, place, merge_gain))
    turn, gains = call(
        residual_kernel,
        (sds((VD // 2 + 2 * UNITS, VD // 2), bf16), sds((1, VD), f32)),
        (place, patches, merge_gain.reshape(1, VD)),
        [SMEM] + [VMEM] * 2,
    )
    partial = lax.all_to_all(
        partial.reshape(NX, UNITS, VD), "head", split_axis=0, concat_axis=0, tiled=True
    ).reshape(FPATCH, VD)
    partial, far, gains, turn = barrier((partial, far, gains, turn))
    far_other = lax.ppermute(far, "seq_2", [(0, 1), (1, 0)])
    merged = call(merge_kernel, sds((UNITS, VD), bf16), (place, partial, gains, turn), [SMEM] + [VMEM] * 3)
    merged = lax.all_gather(merged, "head", axis=0, tiled=True)
    visual = call(visual_kernel, sds((LAYER, UNITS, 512), bf16), (merged, far, far_other), vmem=24 << 20)
    asked = far[:, -16:-8].reshape(NZ * 8, 512)
    visual = lax.all_to_all(
        visual, ("seq_1", "seq_2"), split_axis=0, concat_axis=0, tiled=True
    ).reshape(LAYER * UNITS, 512)
    sent = call(
        attend_kernel,
        sds((NZ * 8, 5 * HD), bf16),
        (place, visual, asked, frame_range),
        [SMEM] + [VMEM] * 3,
    )
    sent, queries, suffix_kv, question_lengths = barrier((sent, queries, suffix_kv, question_lengths))
    got = lax.all_to_all(
        sent.reshape(NZ, 8, 5 * HD), TURNS[0], split_axis=0, concat_axis=0, axis_index_groups=TURNS[1], tiled=True
    ).reshape(-1, 5 * HD)
    mixed, level = call(
        suffix_kernel,
        (sds((4 * GROUP, HD), f32), sds((4 * GROUP, HD), f32)),
        (question_lengths, queries.reshape(8, 512), suffix_kv.reshape(-1, 512)),
        [SMEM] + [VMEM] * 2,
    )
    return call(answer_kernel, sds((2, 2 * GROUP * HD), bf16), (got, mixed, level))


def solution(mesh):
    torus = Mesh(
        mesh.devices.reshape(NZ, NY, NC, NX), ("seq_0", "seq_1", "seq_2", "head")
    )
    in_specs = (
        P(SEQ, None),
        P(),
        P(SEQ, None, "head"),
        P("head", SEQ),
        P(SEQ, None),
        P(),
        P(SEQ, None, "head"),
        P(SEQ, "head"),
        P(SEQ, None, None, "head"),
        P(SEQ),
        P(),
    )
    return jax.shard_map(
        on_device, mesh=torus, in_specs=in_specs, out_specs=P(SEQ, "head"), check_vma=False
    )
```

```python
import jax
import jax.numpy as jnp
from jax import lax
from jax.experimental import pallas as pl
from jax.experimental.pallas import tpu as pltpu
from jax.sharding import Mesh
from jax.sharding import PartitionSpec as P

VD = 1280
VH = 16
HD = 128
FPATCH = 256
WIN = 64
SEQ = ("seq_0", "seq_1", "seq_2")
NZ, NY, NC, NX = 16, 4, 2, 4
ROWS = VD // (NZ * NY * NC)
PACKED = 24
COLS = VD // NX
HEAD = VD // VH
HEADS = COLS // HEAD
UNITS = FPATCH // 4
GROUP = 8
LAYER = NY * NC
NEGATIVE = -1e30
f32 = jnp.float32
bf16 = jnp.bfloat16


def dot(a, b):
    return lax.dot_general(a, b, (((1,), (0,)), ((), ())), preferred_element_type=f32)


def dot_t(a, b):
    return lax.dot_general(a, b, (((1,), (1,)), ((), ())), preferred_element_type=f32)


def iota(shape, dim):
    return lax.broadcasted_iota(jnp.int32, shape, dim)


def one_hot(condition):
    return jnp.where(condition, 1.0, 0.0).astype(bf16)


def call(body, outs, operands, specs=None, vmem=24 << 20):
    vm = pl.BlockSpec(memory_space=pltpu.VMEM)
    return pl.pallas_call(
        body,
        out_shape=outs,
        in_specs=specs or [vm] * len(operands),
        out_specs=jax.tree.map(lambda _: vm, outs),
        compiler_params=pltpu.CompilerParams(vmem_limit_bytes=vmem),
    )(*operands)


VMEM = pl.BlockSpec(memory_space=pltpu.VMEM)
SMEM = pl.BlockSpec(memory_space=pltpu.SMEM)


def places():
    at = iota((VD, 1), 0)
    return at // (NY * NC * ROWS), at // (NC * ROWS) % NY, at // ROWS % NC, at % ROWS


def prepare_kernel(place_ref, patches_ref, gain_ref, window_ref, normed_ref, member_ref):
    order = one_hot(iota((VD, VD), 1) == gathered(place_ref[2]))
    source = patches_ref[...].astype(f32)
    scale = lax.rsqrt(jnp.mean(source * source, axis=-1, keepdims=True) + 1e-06)
    normed = (source * scale * gain_ref[...]).astype(bf16)
    normed_ref[...] = dot(normed, order).astype(bf16)
    member = one_hot(window_ref[...] == iota((FPATCH, UNITS), 0) // 4)
    shape = (UNITS, 128)
    member_ref[...] = dot(member, one_hot(iota(shape, 0) // (WIN // 4) == iota(shape, 1))).astype(bf16)


def gathered(core):
    z, y, c, r = places()
    return ((c + core) % NC) * (VD // NC) + (y * NZ + z) * ROWS + r


def residual_kernel(place_ref, patches_ref, gain_ref, turn_ref, gains_ref):
    core = place_ref[2]
    half = VD // 2
    z, y, c, r = places()
    target = (y // 2) * half + (((c + core) % NC * 2 + y % 2) * NZ + z) * ROWS + r
    order = one_hot(iota((VD, VD), 1) == target)
    shape = (UNITS, FPATCH)
    pick = one_hot(iota(shape, 1) == iota(shape, 0) * 4 + place_ref[3])
    source = dot(dot(pick, patches_ref[...]).astype(bf16), order).astype(bf16)
    turn_ref[half : half + UNITS] = source[:, :half]
    turn_ref[half + UNITS :] = source[:, half:]
    gain = gain_ref[...]
    high = gain.astype(bf16).astype(f32)
    middle = (gain - high).astype(bf16).astype(f32)
    low = gain - high - middle
    part = iota((8, 1), 0)
    parts = jnp.where(part == 0, high, jnp.where(part == 1, middle, jnp.where(part == 2, low, 0.0)))
    gains_ref[...] = jnp.sum(dot(parts.astype(bf16), order), axis=0, keepdims=True)
    row = iota((half, 1), 0)
    c, y, z, r = row // (2 * NZ * ROWS), row // (NZ * ROWS) % 2, row // ROWS % NZ, row % ROWS
    target = ((z * 2 + y) * NC + (c + core) % NC) * ROWS + r
    turn_ref[:half] = one_hot(iota((half, half), 1) == target)


def side_by_side(value):
    return jnp.concatenate([value[:, b * HD : (b + 1) * HD] for b in range(4)], axis=0)


def suffix_kernel(length_ref, asking_ref, suffix_ref, mixed_ref, level_ref):
    asking = side_by_side(asking_ref[...])
    count = asking.shape[0]
    span = suffix_ref.shape[0] // 2
    row = iota((count, 1), 0)
    even = row % 4 < 2
    second = row // 4 % 2
    scores = jnp.where(even, dot_t(asking, suffix_ref[:, 0:128]), dot_t(asking, suffix_ref[:, 128:256]))
    col = iota((1, 2 * span), 1)
    length = jnp.where(second == 0, length_ref[0], length_ref[1])
    live = (col // span == second) & (col % span < length)
    scores = jnp.where(live, scores * HD ** (-0.5), NEGATIVE)
    highest = jnp.max(scores, axis=-1, keepdims=True)
    weights = jnp.exp(scores - highest)
    total = jnp.sum(weights, axis=-1, keepdims=True)
    weights = weights.astype(bf16)
    mixed_ref[...] = jnp.where(even, dot(weights, suffix_ref[:, 256:384]), dot(weights, suffix_ref[:, 384:512]))
    level_ref[...] = jnp.where(iota((1, HD), 1) == 0, highest, total)


def compact_kernel(got_ref, weights_ref):
    got = got_ref[...]
    shape = (NZ * ROWS, NZ * PACKED)
    row, col = iota(shape, 0), iota(shape, 1)
    for half in range(2):
        pick = one_hot(col == (row // ROWS) * PACKED + half * ROWS + row % ROWS)
        weights = dot(pick, got).astype(bf16)
        for k in range(NY):
            weights_ref[k, :, half * 640 : (half + 1) * 640] = weights


def vision_kernel(normed_ref, own_ref, other_ref, member_ref, out_ref):
    half = VD // 2
    projected = dot(normed_ref[:, :half], own_ref[:, :1024]) + dot(normed_ref[:, half:], other_ref[:, :1024])
    projected = projected.astype(bf16).astype(f32)
    query = pltpu.roll(projected[:, 0:384], 64, 1)
    key = projected[:, 256:640].astype(bf16)
    value = projected[:, 640:1024]
    together = dot_t(member_ref[...], member_ref[...]) > 0.5
    lane = iota((1, 384), 1)
    mixed = jnp.zeros((FPATCH, 384), f32)
    for h in range(HEADS):
        at = 64 + h * HEAD
        asking = jnp.where((lane >= at) & (lane < at + HEAD), query, 0.0).astype(bf16)
        scores = dot_t(asking, key) * HEAD ** (-0.5)
        scores = jnp.where(together, scores, NEGATIVE)
        weights = jnp.exp(scores - jnp.max(scores, axis=-1, keepdims=True))
        weights = (weights / jnp.sum(weights, axis=-1, keepdims=True)).astype(bf16)
        at = h * HEAD
        mixed += dot(weights, jnp.where((lane >= at) & (lane < at + HEAD), value, 0.0).astype(bf16))
    mixed = pltpu.roll(mixed, 64, 1).astype(bf16)
    shape = (FPATCH, FPATCH)
    row, col = iota(shape, 0), iota(shape, 1)
    mixed = dot(one_hot(col == (row % UNITS) * 4 + row // UNITS), mixed).astype(bf16)
    for part in range(2):
        rows = slice(part * half // 2, (part + 1) * half // 2)
        weights = jnp.concatenate([own_ref[rows, 896:1280], other_ref[rows, 896:1280]], axis=0)
        out_ref[:, part * half : (part + 1) * half] = dot_t(mixed, weights).astype(bf16)


def merge_kernel(place_ref, got_ref, gain_ref, turn_ref, out_ref):
    half = VD // 2
    hidden = jnp.concatenate([turn_ref[half : half + UNITS], turn_ref[half + UNITS :]], axis=1).astype(f32)
    for k in range(NX):
        hidden += got_ref[k * UNITS : (k + 1) * UNITS].astype(f32)
    scale = lax.rsqrt(jnp.mean(hidden * hidden, axis=-1, keepdims=True) + 1e-06)
    merged = (hidden * scale * gain_ref[...]).astype(bf16)
    left = dot(merged[:, :half], turn_ref[:half])
    right = dot(merged[:, half:], turn_ref[:half])
    first = place_ref[2] == 0
    out_ref[:, :half] = jnp.where(first, left, right).astype(bf16)
    out_ref[:, half:] = jnp.where(first, right, left).astype(bf16)


def visual_kernel(merged_ref, own_ref, other_ref, out_ref, held_ref, sems):
    rows = 4 * NY * ROWS
    half = VD // 2
    sides = (own_ref, other_ref)

    def copy(side, k):
        return pltpu.make_async_copy(
            sides[side].at[k, pl.ds(0, rows)],
            held_ref.at[pl.ds((side * NZ + k) * rows, rows)],
            sems.at[side * NZ + k],
        )

    for k in range(NZ):
        for side in range(2):
            copy(side, k).start()
    total = jnp.zeros((UNITS, 512), f32)
    for i in range(4):
        for side in range(2):
            for k in range(4):
                copy(side, i * 4 + k).wait()
            merged = merged_ref[i * UNITS : (i + 1) * UNITS, side * half : (side + 1) * half]
            at = (side * 4 + i) * half
            total += dot(merged, held_ref[at : at + half])
    visual = total.astype(bf16)
    for k in range(LAYER):
        out_ref[k] = visual


def attend_kernel(place_ref, visual_ref, asked_ref, range_ref, out_ref):
    layer, inner = place_ref[0], place_ref[1]
    count = NZ * 4 * GROUP
    tokens = LAYER * UNITS
    asking = side_by_side(asked_ref[...])
    row = iota((count, 1), 0)
    even = row % 4 < 2
    question = ((row // 8) % NZ * LAYER + inner) * 2 + (row // 4) % 2
    pick = one_hot(iota((count, 256), 1) == question)
    bounds = dot(pick, range_ref[...].astype(f32).astype(bf16))
    lower, upper = bounds[:, 0:1], bounds[:, 1:2]
    frame = (layer * LAYER + iota((1, tokens), 1) // UNITS).astype(f32)
    live = (frame >= lower) & (frame < upper)
    scores = jnp.where(even, dot_t(asking, visual_ref[:, 0:128]), dot_t(asking, visual_ref[:, 128:256]))
    scores = jnp.where(live, scores * HD ** (-0.5), NEGATIVE)
    highest = jnp.max(scores, axis=-1, keepdims=True)
    weights = jnp.exp(scores - highest)
    total = jnp.sum(weights, axis=-1, keepdims=True)
    weights = weights.astype(bf16)
    mixed = jnp.where(even, dot(weights, visual_ref[:, 256:384]), dot(weights, visual_ref[:, 384:512]))
    mixed = mixed / total
    level = highest + jnp.log(total)
    high = level.astype(bf16).astype(f32)
    middle = (level - high).astype(bf16).astype(f32)
    low = level - high - middle
    lane = iota((1, HD), 1)
    block = row // (NZ * 8)
    levels = jnp.where(
        lane == block, high, jnp.where(lane == block + 4, middle, jnp.where(lane == block + 8, low, 0.0))
    )
    blocks = [slice(b * NZ * 8, (b + 1) * NZ * 8) for b in range(4)]
    for b in range(4):
        out_ref[:, b * HD : (b + 1) * HD] = mixed[blocks[b]].astype(bf16)
    out_ref[:, 4 * HD :] = sum(levels[at] for at in blocks).astype(bf16)


def answer_kernel(got_ref, mixed_ref, level_ref, out_ref):
    got = got_ref[...].astype(f32)
    count = 8
    lane = iota((1, HD), 1)
    answers = []
    for b in range(4):
        at = slice(b * count, (b + 1) * count)
        highest, total = level_ref[at, 0:1], level_ref[at, 1:2]
        mine = (lane < 12) & (lane % 4 == b)
        level = jnp.sum(jnp.where(mine, got[:, 4 * HD :], 0.0), axis=-1, keepdims=True)
        levels = [level[k * count : (k + 1) * count] for k in range(NZ)]
        top = highest
        for k in range(NZ):
            top = jnp.maximum(top, levels[k])
        share = jnp.exp(highest - top)
        mixed = mixed_ref[at] * share
        total = total * share
        for k in range(NZ):
            share = jnp.exp(levels[k] - top)
            mixed += got[k * count : (k + 1) * count, b * HD : (b + 1) * HD] * share
            total += share
        answers.append(mixed / total)
    answers = jnp.concatenate(answers, axis=1)
    for a in range(4):
        pair = jnp.concatenate([answers[a : a + 1], answers[4 + a : 5 + a]], axis=0)
        out_ref[:, a * 512 : (a + 1) * 512] = pair.astype(bf16)


def on_device(
    patches,
    norm_gain,
    w_qkv,
    w_out,
    window_order,
    merge_gain,
    w_kv,
    queries,
    suffix_kv,
    question_lengths,
    frame_range,
):
    sds = jax.ShapeDtypeStruct
    barrier = lax.optimization_barrier
    layer = lax.axis_index("seq_0")
    inner = lax.axis_index(("seq_1", "seq_2"))
    place = jnp.stack([layer, inner, lax.axis_index("seq_2"), lax.axis_index("head")])

    near = jnp.broadcast_to(w_kv[None], (NY, *w_kv.shape))
    near = lax.all_to_all(near, "seq_1", split_axis=0, concat_axis=0, tiled=True).reshape(-1, 512)
    packed = jnp.concatenate([w_qkv.reshape(ROWS, 3 * COLS), w_out.T], axis=1)
    packed = jnp.concatenate(
        [packed[:, :640], packed[:, 640:], jnp.zeros((PACKED - 2 * ROWS, 640), bf16)], axis=0
    )
    packed, near = barrier((packed, near))
    near = jnp.concatenate([near, queries.reshape(8, 512), jnp.zeros((8, 512), bf16)], axis=0)
    far = lax.all_gather(near, "seq_0", axis=0)
    got = lax.all_gather(packed, "seq_0", axis=0, tiled=True)
    weights = call(compact_kernel, sds((NY, NZ * ROWS, VD), bf16), (got,))

    weights, patches, place, norm_gain, window_order = barrier((weights, patches, place, norm_gain, window_order))
    normed, member = call(
        prepare_kernel,
        (sds((FPATCH, VD), bf16), sds((FPATCH, 128), bf16)),
        (place, patches, norm_gain.reshape(1, VD), window_order),
        [SMEM] + [VMEM] * 3,
    )
    own = lax.all_to_all(weights, "seq_1", split_axis=0, concat_axis=0, tiled=True).reshape(VD // 2, VD)
    own, normed, member = barrier((own, normed, member))
    other = lax.ppermute(own, "seq_2", [(0, 1), (1, 0)])
    partial = call(
        vision_kernel, sds((FPATCH, VD), bf16), (normed, own, other, member)
    )

    partial, patches, place, merge_gain = barrier((partial, patches, place, merge_gain))
    turn, gains = call(
        residual_kernel,
        (sds((VD // 2 + 2 * UNITS, VD // 2), bf16), sds((1, VD), f32)),
        (place, patches, merge_gain.reshape(1, VD)),
        [SMEM] + [VMEM] * 2,
    )
    partial = lax.all_to_all(
        partial.reshape(NX, UNITS, VD), "head", split_axis=0, concat_axis=0, tiled=True
    ).reshape(FPATCH, VD)
    partial, far, gains, turn = barrier((partial, far, gains, turn))
    far_other = lax.ppermute(far, "seq_2", [(0, 1), (1, 0)])
    merged = call(merge_kernel, sds((UNITS, VD), bf16), (place, partial, gains, turn), [SMEM] + [VMEM] * 3)
    merged = lax.all_gather(merged, "head", axis=0, tiled=True)
    anywhere = pl.BlockSpec(memory_space=pl.ANY)
    visual = pl.pallas_call(
        visual_kernel,
        out_shape=sds((LAYER, UNITS, 512), bf16),
        in_specs=[VMEM, anywhere, anywhere],
        out_specs=VMEM,
        scratch_shapes=[pltpu.VMEM((4 * VD, 512), bf16), pltpu.SemaphoreType.DMA((2 * NZ,))],
        compiler_params=pltpu.CompilerParams(vmem_limit_bytes=58 << 20),
    )(merged, far, far_other)
    asked = far[:, -16:-8].reshape(NZ * 8, 512)
    visual = lax.all_to_all(
        visual, ("seq_1", "seq_2"), split_axis=0, concat_axis=0, tiled=True
    ).reshape(LAYER * UNITS, 512)
    sent = call(
        attend_kernel,
        sds((NZ * 8, 5 * HD), bf16),
        (place, visual, asked, frame_range),
        [SMEM] + [VMEM] * 3,
    )
    sent, queries, suffix_kv, question_lengths = barrier((sent, queries, suffix_kv, question_lengths))
    got = lax.all_to_all(
        sent.reshape(NZ, 8, 5 * HD), "seq_0", split_axis=0, concat_axis=0, tiled=True
    ).reshape(-1, 5 * HD)
    mixed, level = call(
        suffix_kernel,
        (sds((4 * GROUP, HD), f32), sds((4 * GROUP, HD), f32)),
        (question_lengths, queries.reshape(8, 512), suffix_kv.reshape(-1, 512)),
        [SMEM] + [VMEM] * 2,
    )
    return call(answer_kernel, sds((2, 2 * GROUP * HD), bf16), (got, mixed, level))


def solution(mesh):
    torus = Mesh(
        mesh.devices.reshape(NZ, NY, NC, NX), ("seq_0", "seq_1", "seq_2", "head")
    )
    in_specs = (
        P(SEQ, None),
        P(),
        P(SEQ, None, "head"),
        P("head", SEQ),
        P(SEQ, None),
        P(),
        P(SEQ, None, "head"),
        P(SEQ, "head"),
        P(SEQ, None, None, "head"),
        P(SEQ),
        P(),
    )
    return jax.shard_map(
        on_device, mesh=torus, in_specs=in_specs, out_specs=P(SEQ, "head"), check_vma=False
    )
```
